32 devices in a mesh: dp: 16 (over z, y, x), tensor: 2 (over core).
Axes of the slice: x: 2, y: 2, z: 4, core: 2. Of those that a mesh axis runs over, the one named last changes fastest.
Arguments:
- grad_out: bfloat16 [12288, 4096], P(('dp', 'tensor')), may hold values from -0.109375 to 0.109375
- activations: bfloat16 [12288, 14336], P('dp', 'tensor'), may hold values from -6 to 6
- grad_dither: float32 [12288, 4096], P(('dp', 'tensor')), may hold values from -0.5 to 0.5
- hidden_dither: float32 [16, 14336], P('dp', 'tensor'), may hold values from -0.25 to 0.25
- feature_dither: float32 [16, 4096], P('dp'), may hold values from -0.25 to 0.25
Outputs:
- weight_grad: float32 [4096, 14336], P('dp', 'tensor')
The draws below stay inside these ranges and needn't reach their ends.
All inputs are finite; a program needn't handle non-finite values.
Results may differ from the reference program's by a relative error of at most 0.014.
Values may be sent and summed in bfloat16 or wider, within the bound.
No kernel may reach another device: no remote copies, remote signals or barrier semaphores. Data moves between devices by JAX's collectives and lax.ppermute only.
A program may use at most 192 MiB of HBM per device.

```python
import jax
import jax.numpy as jnp
from jax import lax

D = 4096
FF_WIN = 14336
TOK = 768
BLOCK = 128
Y_LEVELS = 8
W_LEVELS = 7
TOKENS = 12288
N_DP = 16


def raised(result, rng, source, target, blocks, factor):
    def block_of(dim):
        return (jnp.arange(result.shape[dim]) // (result.shape[dim] // blocks)).reshape((-1,) + (1,) * (result.ndim - 1 - dim))

    near = jax.random.permutation(rng, blocks)[block_of(target)]
    other_side = (block_of(target) + blocks // 2) % blocks
    return jnp.where((block_of(source) == near) | (block_of(source) == other_side), factor * result, result)


def steps_of(stream_key, extent, split, least, top_value):
    factor_of, own = 1.0, jax.random.fold_in(stream_key, 6)
    for position, blocks in split:
        steps = jnp.exp(jax.random.uniform(jax.random.fold_in(own, position), (blocks,), jnp.float32, least / len(split), top_value / len(split)))
        factor_of = factor_of * jnp.repeat(steps, extent[position] // blocks).reshape([-1 if axis == position else 1 for axis in range(len(extent))])
    return factor_of


def gaussian(own_key, dims, width, most, pieces=(), dtype=jnp.bfloat16):
    values = jax.random.normal(own_key, dims, jnp.float32) * width
    if len(pieces) > 0:
        values = steps_of(own_key, dims, pieces, -0.22, 0.18) * values
    return jnp.clip(values, min=-most, max=most).astype(dtype)


def gaussian_with(key, shape, spread, reach, split, heavy, held_as=jnp.bfloat16):
    result = spread * jax.random.normal(key, shape, jnp.float32)
    if split:
        result = result * steps_of(key, shape, split, -0.22, 0.18)
    return jnp.clip(raised(result, jax.random.fold_in(key, 3), *heavy), -reach, reach).astype(held_as)


def setup_inputs(seed: int = 0) -> dict:
    splits = jax.random.split(jax.random.key(seed), 6)
    grad_out = gaussian_with(splits[0], (TOKENS, D), (TOK * N_DP) ** -0.5, 0.109375, ((0, 32),), (0, 1, 32, 2.75))
    activations = gaussian(splits[1], (TOKENS, FF_WIN), 1.0, 6.0, ((0, 16), (1, 2)))
    grad_dither = jnp.clip(jax.random.uniform(splits[2], (TOKENS, D), jnp.float32, -0.5, 0.5) * steps_of(splits[2], (TOKENS, D), ((0, 32),), -0.4, 0.0), -0.5, 0.5)
    hidden_dither = jnp.clip(jax.random.uniform(splits[3], (N_DP, FF_WIN), jnp.float32, -0.25, 0.25) * steps_of(splits[3], (N_DP, FF_WIN), ((0, 16), (1, 2)), -0.4, 0.0), -0.25, 0.25)
    feature_dither = jnp.clip(jax.random.uniform(splits[4], (N_DP, D), jnp.float32, -0.25, 0.25) * steps_of(splits[4], (N_DP, D), ((0, 16),), -0.4, 0.0), -0.25, 0.25)
    return {"grad_out": grad_out, "activations": activations, "grad_dither": grad_dither, "hidden_dither": hidden_dither, "feature_dither": feature_dither}


epsilon = 1e-6


def decode_rows(code_rows, scale_rows):
    row_total = code_rows.shape[0]
    block_count = code_rows.shape[1] // BLOCK
    held = lax.optimization_barrier(code_rows).astype(jnp.float32)
    values = held.reshape(row_total, block_count, BLOCK) * scale_rows.astype(jnp.float32)[:, :, None]
    return values.reshape(row_total, block_count * BLOCK).astype(jnp.bfloat16)


def decode_terms(code_block, block_scale):
    feat_rows, unit_cols = code_block.shape
    block_count = feat_rows // BLOCK
    held = lax.optimization_barrier(code_block).astype(jnp.float32)
    values = held.reshape(block_count, BLOCK, unit_cols) * block_scale.astype(jnp.float32)[:, None, :]
    return values.reshape(feat_rows, unit_cols).astype(jnp.bfloat16)


def quantize(partial_value, feature_part, hidden_part):
    feat_rows, unit_cols = partial_value.shape
    block_count = feat_rows // BLOCK
    blocks = partial_value.reshape(block_count, BLOCK, unit_cols)
    magnitude = jnp.max(jnp.abs(blocks), axis=1)
    block_scale = ((magnitude + epsilon) / W_LEVELS).astype(jnp.bfloat16)
    scaled = (blocks / block_scale.astype(jnp.float32)[:, None, :]).reshape(feat_rows, unit_cols)
    code_block = (scaled + hidden_part[None, :] + feature_part[:, None]).astype(jnp.bfloat16)
    return code_block, block_scale


def reference(grad_out, activations, grad_dither, hidden_dither, feature_dither):
    grad_float = grad_out.astype(jnp.float32)
    row_total = grad_out.shape[0]
    block_count = D // BLOCK
    magnitude = jnp.max(jnp.abs(grad_float).reshape(row_total, block_count, BLOCK), axis=2)
    y_scale = ((magnitude + epsilon) / Y_LEVELS).astype(jnp.bfloat16)
    scaled = grad_float.reshape(row_total, block_count, BLOCK) / y_scale.astype(jnp.float32)[:, :, None]
    y_code = (scaled.reshape(row_total, D) + grad_dither).astype(jnp.bfloat16)
    y_hat = decode_rows(y_code, y_scale)

    def group_term(grad_total, inputs):
        y_group, act_group, hidden_part, feature_part = inputs
        partial_value = lax.dot_general(y_group, act_group, (((0,), (0,)), ((), ())), preferred_element_type=jnp.float32)
        code_block, block_scale = quantize(partial_value, feature_part, hidden_part)
        term = decode_terms(code_block, block_scale)
        held = lax.optimization_barrier(term).astype(jnp.float32)
        return grad_total + held, None

    inputs = (y_hat.reshape(N_DP, TOK, D), activations.reshape(N_DP, TOK, FF_WIN), hidden_dither, feature_dither)
    weight_grad, unused = lax.scan(group_term, jnp.zeros((D, FF_WIN), jnp.float32), inputs)
    return weight_grad
```

```python
import jax
import jax.numpy as jnp
from jax import lax
from jax.experimental import pallas as pl
from jax.experimental.pallas import tpu as pltpu
from jax.sharding import PartitionSpec as P

BLOCK = 128
Y_LEVELS = 8
W_LEVELS = 7
EPSILON = 1e-06
LANES = 128
VMEM_LIMIT = 40 * 1024 * 1024

CHUNKS = (1, 1, 2, 2, 2, 2, 2, 1, 1)
LATE_FIRST = (1, 4)


def code_rows_kernel(order_ref, grad_ref, dither_ref, out_ref):
    for start in range(0, grad_ref.shape[1], BLOCK):
        grad = grad_ref[:, start : start + BLOCK].astype(jnp.float32)
        top = jnp.max(jnp.abs(grad), axis=1, keepdims=True)
        scale = ((top + EPSILON) / Y_LEVELS).astype(jnp.bfloat16).astype(jnp.float32)
        value = grad + dither_ref[:, start : start + BLOCK] * scale
        out_ref[0, start : start + BLOCK, :] = value.T.astype(jnp.bfloat16)


def code_rows(order, grad_out, grad_dither, own_rows):
    row_count = grad_out.shape[0]
    steps = order.shape[0]
    spec = pl.BlockSpec((row_count, own_rows), lambda i, order: (0, order[i]))
    return pl.pallas_call(
        code_rows_kernel,
        grid_spec=pltpu.PrefetchScalarGridSpec(
            num_scalar_prefetch=1,
            grid=(steps,),
            in_specs=[spec, spec],
            out_specs=pl.BlockSpec((1, own_rows, row_count), lambda i, order: (i, 0, 0)),
        ),
        out_shape=jax.ShapeDtypeStruct((steps, own_rows, row_count), jnp.bfloat16),
        compiler_params=pltpu.CompilerParams(vmem_limit_bytes=VMEM_LIMIT),
    )(order, grad_out, grad_dither)


def group_terms(y_block, acts, hidden, feature):
    partial = jnp.dot(y_block, acts, preferred_element_type=jnp.float32)
    wide = jnp.concatenate([feature] * (acts.shape[1] // LANES), axis=1)
    out = []
    for start in range(0, y_block.shape[0], BLOCK):
        piece = partial[start : start + BLOCK]
        top = jnp.max(jnp.abs(piece), axis=0, keepdims=True)
        scale = ((top + EPSILON) / W_LEVELS).astype(jnp.bfloat16).astype(jnp.float32)
        out.append(piece + (wide[start : start + BLOCK] + hidden) * scale)
    return out


def pair_terms_kernel(
    order_ref, y0_ref, y1_ref, a0_ref, a1_ref, h0_ref, h1_ref, f0_ref, f1_ref, send_ref, keep_ref
):
    step = pl.program_id(0)
    half = pl.num_programs(0) // 2
    mine = group_terms(y0_ref[0], a0_ref[...], h0_ref[...], f0_ref[0])
    other = group_terms(y1_ref[0], a1_ref[...], h1_ref[...], f1_ref[0])
    total = jnp.concatenate([a + b for a, b in zip(mine, other)], axis=0).astype(jnp.bfloat16)

    @pl.when(step < half)
    def _():
        send_ref[0] = total

    @pl.when(step >= half)
    def _():
        keep_ref[0] = total


def pair_terms(order, y0, y1, acts, start, width, acts1, h0, h1, f0, f1):
    steps, own_rows, tokens = y0.shape
    half = steps // 2
    y_spec = pl.BlockSpec((1, own_rows, tokens), lambda i, order: (order[i], 0, 0))
    f_spec = pl.BlockSpec((1, own_rows, LANES), lambda i, order: (order[i], 0, 0))
    at = start // width
    out = jax.ShapeDtypeStruct((half, own_rows, width), jnp.bfloat16)
    return pl.pallas_call(
        pair_terms_kernel,
        grid_spec=pltpu.PrefetchScalarGridSpec(
            num_scalar_prefetch=1,
            grid=(steps,),
            in_specs=[
                y_spec,
                y_spec,
                pl.BlockSpec((tokens, width), lambda i, order: (0, at)),
                pl.BlockSpec((tokens, width), lambda i, order: (0, 0)),
                pl.BlockSpec((1, width), lambda i, order: (0, 0)),
                pl.BlockSpec((1, width), lambda i, order: (0, 0)),
                f_spec,
                f_spec,
            ],
            out_specs=[
                pl.BlockSpec(
                    (1, own_rows, width), lambda i, order: (jnp.minimum(i, half - 1), 0, 0)
                ),
                pl.BlockSpec(
                    (1, own_rows, width), lambda i, order: (jnp.maximum(i - half, 0), 0, 0)
                ),
            ],
        ),
        out_shape=[out, out],
        compiler_params=pltpu.CompilerParams(vmem_limit_bytes=VMEM_LIMIT),
        cost_estimate=pl.CostEstimate(
            flops=4 * steps * own_rows * tokens * width,
            bytes_accessed=4 * steps * own_rows * tokens + 2 * steps * own_rows * width + 4 * tokens * width,
            transcendentals=0,
        ),
    )(order, y0, y1, acts, acts1, h0, h1, f0, f1)


def bits_of(count):
    return [1 << i for i in range(count.bit_length() - 1)]


def relative_order(bits):
    order = [0]
    for bit in reversed(bits):
        order = order + [bit | r for r in order]
    return order


def per_device(grad_out, activations, grad_dither, hidden_dither, feature_dither):
    owners = lax.axis_size("dp")
    feat_width = grad_out.shape[1]
    own_rows = feat_width // owners
    unit_count = activations.shape[1]
    me = lax.axis_index("dp").astype(jnp.int32)

    def exchange(value, bit):
        return lax.ppermute(value, "dp", [(i, i ^ bit) for i in range(owners)])

    pair_bit, *rest = bits_of(owners)
    unit = unit_count // sum(CHUNKS)
    widths = [c * unit for c in CHUNKS]
    starts = [sum(widths[:k]) for k in range(len(widths))]

    rel = relative_order(rest)
    rel_index = jnp.array(rel, jnp.int32)
    y_send = code_rows(rel_index ^ (me ^ pair_bit), grad_out, grad_dither, own_rows)
    y_mine = code_rows(rel_index ^ me, grad_out, grad_dither, own_rows)
    y_other = exchange(y_send, pair_bit)
    y0 = lax.all_gather(y_mine, "tensor", axis=2, tiled=True)
    y1 = lax.all_gather(y_other, "tensor", axis=2, tiled=True)
    hidden_other = exchange(hidden_dither, pair_bit)
    feature_other = exchange(feature_dither, pair_bit)

    def feature_column(values):
        picked = values.reshape(owners, own_rows)[rel_index ^ me]
        return jnp.broadcast_to(picked[:, :, None], (owners // 2, own_rows, LANES))

    f0, f1 = feature_column(feature_dither), feature_column(feature_other)

    outs = []
    for k, (start, width) in enumerate(zip(starts, widths)):
        bits = [rest[1], rest[0], *rest[2:]] if k in LATE_FIRST else rest
        wanted = relative_order(bits)
        wanted = wanted[len(wanted) // 2 :] + wanted[: len(wanted) // 2]
        order = jnp.array([rel.index(r) for r in wanted], jnp.int32)
        acts_other = exchange(activations[:, start : start + width], pair_bit)
        send, keep = pair_terms(
            order, y0, y1, activations, start, width, acts_other,
            hidden_dither[:, start : start + width], hidden_other[:, start : start + width], f0, f1,
        )
        held = [keep]
        for at, bit in enumerate(bits):
            held.append(exchange(send, bit))
            count = held[0].shape[0] // 2
            if count:
                send = sum(h[count : 2 * count].astype(jnp.float32) for h in held).astype(jnp.bfloat16)
                held = [h[:count] for h in held]
        outs.append(sum(h[0].astype(jnp.float32) for h in held))
    return jnp.concatenate(outs, axis=1)


def solution(mesh):
    placed = (
        P(("dp", "tensor"), None),
        P("dp", "tensor"),
        P(("dp", "tensor"), None),
        P("dp", "tensor"),
        P("dp", None),
    )
    return jax.shard_map(
        per_device, mesh=mesh, in_specs=placed, out_specs=P("dp", "tensor"), check_vma=False
    )
```

```python
import jax
import jax.numpy as jnp
from jax import lax
from jax.experimental import pallas as pl
from jax.experimental.pallas import tpu as pltpu
from jax.sharding import PartitionSpec as P

BLOCK = 128
Y_LEVELS = 8
W_LEVELS = 7
EPSILON = 1e-06
LANES = 128
VMEM_LIMIT = 56 * 1024 * 1024

CHUNKS = ((1, 0), (1, 1), (2, 0), (2, 0), (2, 1), (2, 0), (2, 0), (1, 0), (1, 0))
SMALL_COST = pl.CostEstimate(flops=1, bytes_accessed=1, transcendentals=0)
ANYWHERE = pl.BlockSpec(memory_space=pl.ANY)


def params():
    return pltpu.CompilerParams(vmem_limit_bytes=VMEM_LIMIT)


def code_rows_kernel(grad_ref, dither_ref, out_ref):
    for start in range(0, grad_ref.shape[1], BLOCK):
        grad = grad_ref[:, start : start + BLOCK].astype(jnp.float32)
        top = jnp.max(jnp.abs(grad), axis=1, keepdims=True)
        scale = ((top + EPSILON) / Y_LEVELS).astype(jnp.bfloat16).astype(jnp.float32)
        value = grad + dither_ref[:, start : start + BLOCK] * scale
        out_ref[0, start : start + BLOCK, :] = value.T.astype(jnp.bfloat16)


def code_rows(order, grad_out, grad_dither, own_rows, after=()):
    row_count = grad_out.shape[0]
    steps = order.shape[0]
    spec = pl.BlockSpec((row_count, own_rows), lambda i, order: (0, order[i]))

    def body(order_ref, grad_ref, dither_ref, *rest):
        code_rows_kernel(grad_ref, dither_ref, rest[-1])

    return pl.pallas_call(
        body,
        grid_spec=pltpu.PrefetchScalarGridSpec(
            num_scalar_prefetch=1,
            grid=(steps,),
            in_specs=[spec, spec] + [ANYWHERE] * len(after),
            out_specs=pl.BlockSpec((1, own_rows, row_count), lambda i, order: (i, 0, 0)),
        ),
        out_shape=jax.ShapeDtypeStruct((steps, own_rows, row_count), jnp.bfloat16),
        compiler_params=params(),
        cost_estimate=SMALL_COST,
    )(order, grad_out, grad_dither, *after)


def cut_columns(values, start, width, after=()):
    rows = values.shape[0]
    steps = 4 if rows % 64 == 0 else 1
    at = start // width

    def body(in_ref, *rest):
        rest[-1][...] = in_ref[...]

    return pl.pallas_call(
        body,
        grid=(steps,),
        in_specs=[pl.BlockSpec((rows // steps, width), lambda i: (i, at))] + [ANYWHERE] * len(after),
        out_specs=pl.BlockSpec((rows // steps, width), lambda i: (i, 0)),
        out_shape=jax.ShapeDtypeStruct((rows, width), values.dtype),
        compiler_params=params(),
        cost_estimate=SMALL_COST,
    )(values, *after)


def group_terms(y_block, acts, hidden, feature):
    partial = jnp.dot(y_block, acts, preferred_element_type=jnp.float32)
    wide = jnp.concatenate([feature] * (acts.shape[1] // LANES), axis=1)
    out = []
    for start in range(0, y_block.shape[0], BLOCK):
        piece = partial[start : start + BLOCK]
        top = jnp.max(jnp.abs(piece), axis=0, keepdims=True)
        scale = ((top + EPSILON) / W_LEVELS).astype(jnp.bfloat16).astype(jnp.float32)
        out.append(piece + (wide[start : start + BLOCK] + hidden) * scale)
    return out


def joined(core, pieces):
    if len(pieces) == 1:
        return pieces[0][0]
    mine, other = (p[0] for p in pieces)
    return jnp.where(
        core == 0, jnp.concatenate([mine, other], axis=1), jnp.concatenate([other, mine], axis=1)
    )


def pair_terms(order, y0, y1, acts, start, width, acts1, h0, h1, f0, f1, ahead, after):
    steps, own_rows = y0[0].shape[:2]
    tokens = acts.shape[0]
    half = steps // 2
    count = len(y0)

    def body(order_ref, *refs):
        refs = list(refs)
        y0_refs, y1_refs = refs[:count], refs[count : 2 * count]
        a0_ref, a1_ref, h0_ref, h1_ref, f0_ref, f1_ref = refs[2 * count : 2 * count + 6]
        outs = refs[2 * count + 6 + len(after) + (1 if ahead else 0) :]
        step = pl.program_id(0)
        core = order_ref[steps]
        mine = group_terms(joined(core, y0_refs), a0_ref[...], h0_ref[...], f0_ref[0])
        other = group_terms(joined(core, y1_refs), a1_ref[...], h1_ref[...], f1_ref[0])
        total = jnp.concatenate([a + b for a, b in zip(mine, other)], axis=0).astype(jnp.bfloat16)

        @pl.when(step < half)
        def _():
            outs[0][0] = total

        @pl.when(step >= half)
        def _():
            outs[1][0] = total

        if ahead:
            outs[2][...] = refs[2 * count + 6][...]

    y_specs = [pl.BlockSpec((1, own_rows, y.shape[2]), lambda i, order: (order[i], 0, 0)) for y in y0]
    f_spec = pl.BlockSpec((1, own_rows, LANES), lambda i, order: (order[i], 0, 0))
    row_spec = pl.BlockSpec((1, width), lambda i, order: (0, 0))
    at = start // width
    out = jax.ShapeDtypeStruct((half, own_rows, width), jnp.bfloat16)
    in_specs = [
        *y_specs,
        *y_specs,
        pl.BlockSpec((tokens, width), lambda i, order: (0, at)),
        pl.BlockSpec((tokens, width), lambda i, order: (0, 0)),
        row_spec,
        row_spec,
        f_spec,
        f_spec,
    ]
    out_specs = [
        pl.BlockSpec((1, own_rows, width), lambda i, order: (jnp.minimum(i, half - 1), 0, 0)),
        pl.BlockSpec((1, own_rows, width), lambda i, order: (jnp.maximum(i - half, 0), 0, 0)),
    ]
    out_shape = [out, out]
    operands = [*y0, *y1, acts, acts1, h0, h1, f0, f1]
    if ahead:
        next_at, next_width = ahead[0] // ahead[1], ahead[1]
        in_specs.append(pl.BlockSpec((tokens // steps, next_width), lambda i, order: (i, next_at)))
        out_specs.append(pl.BlockSpec((tokens // steps, next_width), lambda i, order: (i, 0)))
        out_shape.append(jax.ShapeDtypeStruct((tokens, next_width), acts.dtype))
        operands.append(acts)
    return pl.pallas_call(
        body,
        grid_spec=pltpu.PrefetchScalarGridSpec(
            num_scalar_prefetch=1,
            grid=(steps,),
            in_specs=in_specs + [ANYWHERE] * len(after),
            out_specs=out_specs,
        ),
        out_shape=out_shape,
        compiler_params=params(),
        cost_estimate=SMALL_COST,
    )(order, *operands, *after)


def finish(held, out, unit_count, start, width):
    own_rows = held[0].shape[1]
    at = start // width
    steps = own_rows // LANES
    given = [] if out is None else [out]

    def body(*refs):
        out_ref, token_ref = refs[-2:]
        total = refs[0][0].astype(jnp.float32)
        for ref in refs[1 : len(held)]:
            total = total + ref[0].astype(jnp.float32)
        out_ref[...] = total
        token_ref[...] = total[:8, :LANES]

    return pl.pallas_call(
        body,
        grid=(steps,),
        in_specs=[pl.BlockSpec((1, LANES, width), lambda i: (0, i, 0))] * len(held)
        + [ANYWHERE] * len(given),
        out_specs=[
            pl.BlockSpec((LANES, width), lambda i: (i, at)),
            pl.BlockSpec((8, LANES), lambda i: (0, 0)),
        ],
        out_shape=[
            jax.ShapeDtypeStruct((own_rows, unit_count), jnp.float32),
            jax.ShapeDtypeStruct((8, LANES), jnp.float32),
        ],
        input_output_aliases={len(held): 0} if given else {},
        compiler_params=params(),
        cost_estimate=SMALL_COST,
    )(*held, *given)


def bits_of(count):
    return [1 << i for i in range(count.bit_length() - 1)]


def relative_order(bits):
    order = [0]
    for bit in reversed(bits):
        order = order + [bit | r for r in order]
    return order


def per_device(grad_out, activations, grad_dither, hidden_dither, feature_dither):
    owners = lax.axis_size("dp")
    feat_width = grad_out.shape[1]
    own_rows = feat_width // owners
    unit_count = activations.shape[1]
    me = lax.axis_index("dp").astype(jnp.int32)

    def exchange(value, bit):
        return lax.ppermute(value, "dp", [(i, i ^ bit) for i in range(owners)])

    pair_bit, *rest = bits_of(owners)
    unit = unit_count // sum(c for c, _ in CHUNKS)
    widths = [c * unit for c, _ in CHUNKS]
    starts = [sum(widths[:k]) for k in range(len(widths))]
    spans = list(zip(starts, widths))
    cores = lax.axis_size("tensor")
    core = lax.axis_index("tensor").astype(jnp.int32)

    def over_tokens(values):
        if cores == 2:
            return [values, lax.ppermute(values, "tensor", [(0, 1), (1, 0)])]
        return [lax.all_gather(values, "tensor", axis=2, tiled=True)]

    rel = relative_order(rest)
    rel_index = jnp.array(rel, jnp.int32)
    dithers = jnp.concatenate([hidden_dither, feature_dither], axis=1)
    dithers_other = exchange(dithers, pair_bit)
    hidden_other = dithers_other[:, :unit_count]
    feature_other = dithers_other[:, unit_count:]

    def feature_column(values):
        picked = values.reshape(owners, own_rows)[rel_index ^ me]
        return jnp.broadcast_to(picked[:, :, None], (owners // 2, own_rows, LANES))

    y_send = code_rows(rel_index ^ (me ^ pair_bit), grad_out, grad_dither, own_rows)
    y_other = exchange(y_send, pair_bit)
    acts_cut = cut_columns(activations, *spans[0], after=[y_send])
    acts_other = {0: exchange(acts_cut, pair_bit)}
    y_mine = code_rows(rel_index ^ me, grad_out, grad_dither, own_rows, after=[acts_cut])
    y0 = over_tokens(y_mine)
    acts_cut = cut_columns(activations, *spans[1], after=[y_mine, acts_other[0]])
    acts_other[1] = exchange(acts_cut, pair_bit)
    y1 = over_tokens(y_other)
    f0, f1 = feature_column(feature_dither), feature_column(feature_other)

    held, bits, arrived = {}, {}, {}
    out, after = None, [acts_cut]
    for step in range(len(spans) + len(rest)):
        if step < len(spans):
            start, width = spans[step]
            bits[step] = [rest[1], rest[0], *rest[2:]] if CHUNKS[step][1] else rest
            wanted = relative_order(bits[step])
            wanted = wanted[len(wanted) // 2 :] + wanted[: len(wanted) // 2]
            order = jnp.array([rel.index(r) for r in wanted], jnp.int32)
            order = jnp.concatenate([order, core[None]])
            ahead = spans[step + 2] if step + 2 < len(spans) else None
            send, keep, *cut = pair_terms(
                order, y0, y1, activations, start, width, acts_other.pop(step),
                hidden_dither[:, start : start + width], hidden_other[:, start : start + width],
                f0, f1, ahead, after,
            )
            held[step] = [keep]
            arrived[step] = exchange(send, bits[step][0])
            if ahead:
                acts_other[step + 2] = exchange(cut[0], pair_bit)
            after = [send]
        for stage in range(1, len(rest) + 1):
            chunk = step - stage
            if chunk not in held:
                continue
            held[chunk].append(arrived.pop(chunk))
            parts = held[chunk]
            half = parts[0].shape[0] // 2
            if half:
                send = sum(p[half : 2 * half].astype(jnp.float32) for p in parts).astype(jnp.bfloat16)
                held[chunk] = [p[:half] for p in parts]
                arrived[chunk] = exchange(send, bits[chunk][stage])
                after = after + [send]
            else:
                out, token = finish(held.pop(chunk), out, unit_count, *spans[chunk])
                after = after + [token]
    return out


def solution(mesh):
    placed = (
        P(("dp", "tensor"), None),
        P("dp", "tensor"),
        P(("dp", "tensor"), None),
        P("dp", "tensor"),
        P("dp", None),
    )
    return jax.shard_map(
        per_device, mesh=mesh, in_specs=placed, out_specs=P("dp", "tensor"), check_vma=False
    )
```

```python
import jax
import jax.numpy as jnp
from jax import lax
from jax.experimental import pallas as pl
from jax.experimental.pallas import tpu as pltpu
from jax.sharding import PartitionSpec as P

BLOCK = 128
Y_LEVELS = 8
W_LEVELS = 7
EPSILON = 1e-06
LANES = 128
ADD_ROWS = 64
SMALL_COST = pl.CostEstimate(flops=1, bytes_accessed=1, transcendentals=0)
ANYWHERE = pl.BlockSpec(memory_space=pl.ANY)

CHUNKS = ((2, 0), (4, 2), (6, 2), (6, 2), (6, 2), (6, 2), (6, 2), (4, 2), (2, 0))


def chunks_of(unit_count):
    units = unit_count // LANES
    if units == sum(a + b for a, b in CHUNKS):
        return CHUNKS
    return ((2, 0),) + ((3, 1),) * ((units - 2) // 4) + ((1, 0),) * ((units - 2) % 4)


def params():
    return pltpu.CompilerParams(vmem_limit_bytes=64 * 1024 * 1024)


def code_rows(order, grad_out, grad_dither, own_rows, after=()):
    row_count = grad_out.shape[0]
    steps = order.shape[0]
    spec = pl.BlockSpec((row_count, own_rows), lambda i, order: (0, order[i]))

    def body(order_ref, grad_ref, dither_ref, *rest):
        for start in range(0, own_rows, BLOCK):
            grad = grad_ref[:, start : start + BLOCK].astype(jnp.float32)
            top = jnp.max(jnp.abs(grad), axis=1, keepdims=True)
            scale = ((top + EPSILON) / Y_LEVELS).astype(jnp.bfloat16).astype(jnp.float32)
            value = grad + dither_ref[:, start : start + BLOCK] * scale
            rest[-1][0, start : start + BLOCK, :] = value.T.astype(jnp.bfloat16)

    return pl.pallas_call(
        body,
        grid_spec=pltpu.PrefetchScalarGridSpec(
            num_scalar_prefetch=1,
            grid=(steps,),
            in_specs=[spec, spec] + [ANYWHERE] * len(after),
            out_specs=pl.BlockSpec((1, own_rows, row_count), lambda i, order: (i, 0, 0)),
        ),
        out_shape=jax.ShapeDtypeStruct((steps, own_rows, row_count), jnp.bfloat16),
        compiler_params=params(),
        cost_estimate=SMALL_COST,
    )(order, grad_out, grad_dither, *after)


def cut_columns(values, start, width, after=()):
    def body(in_ref, *rest):
        out_ref, sem = rest[-2:]
        copy = pltpu.make_async_copy(in_ref.at[:, pl.ds(start, width)], out_ref, sem)
        copy.start()
        copy.wait()

    return pl.pallas_call(
        body,
        in_specs=[ANYWHERE] * (1 + len(after)),
        out_specs=ANYWHERE,
        out_shape=jax.ShapeDtypeStruct((values.shape[0], width), values.dtype),
        scratch_shapes=[pltpu.SemaphoreType.DMA],
        compiler_params=params(),
        cost_estimate=SMALL_COST,
    )(values, *after)


def joined(core, pieces):
    if len(pieces) == 1:
        return pieces[0][0]
    mine, other = (p[0] for p in pieces)
    return jnp.where(
        core == 0, jnp.concatenate([mine, other], axis=1), jnp.concatenate([other, mine], axis=1)
    )


def group_terms(y_block, acts, hidden, feature):
    rows, width = y_block.shape[0], acts.shape[1]
    partial = jnp.dot(y_block, acts, preferred_element_type=jnp.float32)
    column = jnp.broadcast_to(feature, (LANES, rows)).T
    wide = jnp.concatenate([column] * (width // LANES), axis=1)
    out = []
    for start in range(0, rows, BLOCK):
        piece = partial[start : start + BLOCK]
        top = jnp.max(jnp.abs(piece), axis=0, keepdims=True)
        scale = ((top + EPSILON) / W_LEVELS).astype(jnp.bfloat16).astype(jnp.float32)
        out.append(piece + (wide[start : start + BLOCK] + hidden) * scale)
    return jnp.concatenate(out, axis=0)


def held_places(writes):
    first = next(w for w in writes if w is not None)
    places = []
    for w in writes:
        places.append(w if w is not None else (places[-1] if places else first))
    return places


def pair_terms(table, y0, y1, acts, acts0, acts1, hidden, feature, start, widths, ahead, after):
    steps, own_rows = y0[0].shape[:2]
    tokens = acts.shape[0]
    half = steps // 2
    count = len(y0)
    width = sum(widths)
    used = [p for p in range(len(widths)) if widths[p]]
    edges = [sum(widths[:p]) for p in range(len(widths))]

    def body(table_ref, *refs):
        refs = list(refs)
        y0_refs, y1_refs = refs[:count], refs[count : 2 * count]
        a0_ref, a1_ref, h0_ref, h1_ref, f0_ref, f1_ref, acts_ref = refs[2 * count : 2 * count + 7]
        outs = refs[2 * count + 7 + len(after) :]
        step = pl.program_id(0)
        core = table_ref[table.shape[0] - 1]
        if ahead:
            cut_ref, sem = outs[2 * len(used) :]
            copy = pltpu.make_async_copy(acts_ref.at[:, pl.ds(*ahead)], cut_ref, sem)

            @pl.when(step == 0)
            def _():
                copy.start()

        columns = slice(start, start + width)
        mine = group_terms(joined(core, y0_refs), a0_ref[...], h0_ref[:, columns], f0_ref[...])
        other = group_terms(joined(core, y1_refs), a1_ref[...], h1_ref[:, columns], f1_ref[...])
        total = (mine + other).astype(jnp.bfloat16)
        for at, p in enumerate(used):
            piece = total[:, edges[p] : edges[p] + widths[p]]
            sends = table_ref[(2 + 3 * p) * steps + step]

            @pl.when(sends == 1)
            def _(at=at, piece=piece):
                outs[2 * at][0] = piece

            @pl.when(sends == 0)
            def _(at=at, piece=piece):
                outs[2 * at + 1][0] = piece

        if ahead:

            @pl.when(step == steps - 1)
            def _():
                copy.wait()

    y_specs = [pl.BlockSpec((1, own_rows, y.shape[2]), lambda i, t: (t[i], 0, 0)) for y in y0]
    f_spec = pl.BlockSpec((1, own_rows), lambda i, t: (0, t[steps + i]))
    a_spec = pl.BlockSpec((tokens, width), lambda i, t: (0, 0))
    h_spec = pl.BlockSpec((1, hidden[0].shape[1]), lambda i, t: (0, 0))
    out_specs, out_shape = [], []
    for p in used:
        for side in range(2):
            row = (3 + 3 * p + side) * steps
            out_specs.append(
                pl.BlockSpec((1, own_rows, widths[p]), lambda i, t, row=row: (t[row + i], 0, 0))
            )
            out_shape.append(jax.ShapeDtypeStruct((half, own_rows, widths[p]), jnp.bfloat16))
    scratch = []
    if ahead:
        out_specs.append(ANYWHERE)
        out_shape.append(jax.ShapeDtypeStruct((tokens, ahead[1]), acts.dtype))
        scratch.append(pltpu.SemaphoreType.DMA)
    return pl.pallas_call(
        body,
        grid_spec=pltpu.PrefetchScalarGridSpec(
            num_scalar_prefetch=1,
            grid=(steps,),
            in_specs=[*y_specs, *y_specs, a_spec, a_spec, h_spec, h_spec, f_spec, f_spec]
            + [ANYWHERE] * (1 + len(after)),
            out_specs=out_specs,
            scratch_shapes=scratch,
        ),
        out_shape=out_shape,
        compiler_params=params(),
        cost_estimate=SMALL_COST,
    )(table, *y0, *y1, acts0, acts1, *hidden, *feature, acts, *after)


def add_up(jobs, result, out_shape, after):
    own_rows = out_shape.shape[0]
    steps = own_rows // ADD_ROWS
    in_specs, operands, out_specs, out_shapes, scratch = [], [], [], [], []
    for parts, owners, start in jobs:
        lead = max(owners, 1)
        for arrays, _ in parts:
            for array, width, column in arrays:
                in_specs.append(
                    pl.BlockSpec(
                        (lead, ADD_ROWS, width),
                        lambda i, o=owners, c=column: (1 if o else 0, i, c),
                    )
                )
                operands.append(array)
        if start is None:
            width = sum(w for _, w in parts)
            out_specs.append(pl.BlockSpec((lead, ADD_ROWS, width), lambda i: (0, i, 0)))
            out_shapes.append(jax.ShapeDtypeStruct((lead, own_rows, width), jnp.bfloat16))
    finals = [(sum(w for _, w in parts), start) for parts, _, start in jobs if start is not None]
    aliases = {}
    if finals:
        if result is not None:
            aliases[len(operands) + len(after)] = len(out_shapes)
        out_specs.append(ANYWHERE)
        out_shapes.append(out_shape)
        scratch = [pltpu.VMEM((ADD_ROWS, finals[0][0]), jnp.float32)]
    given = [result] if aliases else []

    def body(*refs):
        refs = list(refs)
        outs = refs[len(operands) + len(after) + len(given) :]
        step = pl.program_id(0)
        at_in = at_out = 0
        for parts, owners, start in jobs:
            edge = 0
            for arrays, width in parts:
                total = refs[at_in][...].astype(jnp.float32)
                for ref in refs[at_in + 1 : at_in + len(arrays)]:
                    total = total + ref[...].astype(jnp.float32)
                at_in += len(arrays)
                if start is None:
                    outs[at_out][:, :, edge : edge + width] = total.astype(jnp.bfloat16)
                else:
                    outs[-1][:, edge : edge + width] = total[0]
                edge += width
            if start is None:
                at_out += 1
            else:
                pltpu.sync_copy(
                    outs[-1], outs[-2].at[pl.ds(step * ADD_ROWS, ADD_ROWS), pl.ds(start, edge)]
                )

    return pl.pallas_call(
        body,
        grid=(steps,),
        in_specs=in_specs + [ANYWHERE] * (len(after) + len(given)),
        out_specs=out_specs,
        out_shape=out_shapes,
        scratch_shapes=scratch,
        input_output_aliases=aliases,
        compiler_params=params(),
        cost_estimate=SMALL_COST,
    )(*operands, *after, *given)


def bits_of(count):
    return [1 << i for i in range(count.bit_length() - 1)]


def relative_order(bits):
    order = [0]
    for bit in reversed(bits):
        order = order + [bit | r for r in order]
    return order


def per_device(grad_out, activations, grad_dither, hidden_dither, feature_dither):
    owners = lax.axis_size("dp")
    feat_width = grad_out.shape[1]
    own_rows = feat_width // owners
    unit_count = activations.shape[1]
    me = lax.axis_index("dp").astype(jnp.int32)
    cores = lax.axis_size("tensor")
    core = lax.axis_index("tensor").astype(jnp.int32)

    def exchange(value, bit):
        return lax.ppermute(value, "dp", [(i, i ^ bit) for i in range(owners)])

    def over_tokens(values):
        if cores == 2:
            return [values, lax.ppermute(values, "tensor", [(0, 1), (1, 0)])]
        return [lax.all_gather(values, "tensor", axis=2, tiled=True)]

    pair_bit, *rest = bits_of(owners)
    part_bits = [rest, [rest[1], rest[0], *rest[2:]]]
    chunks = chunks_of(unit_count)
    widths = [tuple(LANES * c for c in chunk) for chunk in chunks]
    spans, at = [], 0
    for w in widths:
        spans.append((at, sum(w)))
        at += sum(w)

    rel = relative_order(rest)
    rel = rel[len(rel) // 2 :] + rel[: len(rel) // 2]
    rows = [list(range(len(rel)))]
    part_rows = []
    for bits in part_bits:
        within = relative_order(bits[1:])
        place = [within.index(r & ~bits[0]) for r in rel]
        sends = [1 if r & bits[0] else 0 for r in rel]
        part_rows.append(sends)
        for side in (1, 0):
            part_rows.append(held_places([q if s == side else None for q, s in zip(place, sends)]))
    rel_index = jnp.array(rel, jnp.int32)
    table = jnp.concatenate(
        [jnp.array(rows[0], jnp.int32), rel_index ^ me]
        + [jnp.array(r, jnp.int32) for r in part_rows]
        + [core[None]]
    )

    dithers = jnp.concatenate([hidden_dither, feature_dither], axis=1)
    dithers_other = exchange(dithers, pair_bit)
    hidden = [hidden_dither, dithers_other[:, :unit_count]]
    feature = [feature_dither, dithers_other[:, unit_count:]]
    cuts = {0: cut_columns(activations, *spans[0])}
    acts_other = {0: exchange(cuts[0], pair_bit)}
    y_send = code_rows(rel_index ^ (me ^ pair_bit), grad_out, grad_dither, own_rows, after=[cuts[0]])
    y_other = exchange(y_send, pair_bit)
    y_mine = code_rows(rel_index ^ me, grad_out, grad_dither, own_rows, after=[y_send])
    y0 = over_tokens(y_mine)
    cuts[1] = cut_columns(activations, *spans[1], after=[y_mine, acts_other[0]])
    acts_other[1] = exchange(cuts[1], pair_bit)
    y1 = over_tokens(y_other)

    def terms(chunk, after):
        ahead = spans[chunk + 2] if chunk + 2 < len(spans) else None
        sums = list(pair_terms(
            table, y0, y1, activations, cuts.pop(chunk), acts_other.pop(chunk), hidden, feature,
            spans[chunk][0], widths[chunk], ahead, after,
        ))
        if ahead:
            cuts[chunk + 2] = sums.pop()
        return sums

    stages = len(rest)
    held, sends = {}, {}
    result = None
    out_shape = jax.ShapeDtypeStruct((own_rows, unit_count), jnp.float32)
    made = terms(0, [cuts[1]])
    for step in range(len(spans) + stages - 1):
        arrived = {}
        waits = []
        if step < len(spans):
            used = [p for p in range(2) if widths[step][p]]
            held[step] = {p: [(made[2 * i + 1], widths[step][p], 0)] for i, p in enumerate(used)}
            for i, p in enumerate(used):
                arrived[step, p] = exchange(made[2 * i], part_bits[p][0])
        if step + 2 < len(spans):
            acts_other[step + 2] = exchange(cuts[step + 2], pair_bit)
            waits.append(acts_other[step + 2])
        for key, (send, bit) in sends.items():
            arrived[key] = exchange(send, bit)
        made_before = made
        if step + 1 < len(spans):
            made = terms(step + 1, [s for s, _ in sends.values()] + [made_before[0]])
            waits.append(made[0])
        for (chunk, p), value in arrived.items():
            for q in held[chunk]:
                if p is None or p == q:
                    width = widths[chunk][q]
                    column = 0 if p is not None or q == 0 else widths[chunk][0] // width
                    held[chunk][q].append((value, width, column))
        jobs, keys = [], []
        for chunk in sorted(held):
            stage = step - chunk + 1
            count = len(rel) >> (stage + 1)
            if stage == 1:
                for p, arrays in held[chunk].items():
                    jobs.append(([(arrays, widths[chunk][p])], count, None))
                    keys.append(((chunk, p), part_bits[p][stage]))
            elif count:
                parts = [(arrays, widths[chunk][p]) for p, arrays in held[chunk].items()]
                jobs.append((parts, count, None))
                keys.append(((chunk, None), rest[stage]))
            else:
                parts = [(arrays, widths[chunk][p]) for p, arrays in held[chunk].items()]
                jobs.append((parts, 0, spans[chunk][0]))
        summed = add_up(jobs, result, out_shape, waits)
        if jobs[0][2] is not None:
            result = summed[-1]
            held.pop(min(held))
        sends = {key: (value, bit) for (key, bit), value in zip(keys, summed)}
    return result


def solution(mesh):
    placed = (
        P(("dp", "tensor"), None),
        P("dp", "tensor"),
        P(("dp", "tensor"), None),
        P("dp", "tensor"),
        P("dp", None),
    )
    return jax.shard_map(
        per_device, mesh=mesh, in_specs=placed, out_specs=P("dp", "tensor"), check_vma=False
    )
```

```python
import jax
import jax.numpy as jnp
from jax import lax
from jax.experimental import pallas as pl
from jax.experimental.pallas import tpu as pltpu
from jax.sharding import PartitionSpec as P

BLOCK = 128
Y_LEVELS = 8
W_LEVELS = 7
EPSILON = 1e-06
LANES = 128
ADD_ROWS = 64
SMALL_COST = pl.CostEstimate(flops=1, bytes_accessed=1, transcendentals=0)
ANYWHERE = pl.BlockSpec(memory_space=pl.ANY)

CHUNKS = ((2, 0), (4, 2), (6, 2), (6, 2), (6, 2), (6, 2), (6, 2), (4, 2), (2, 0))


def chunks_of(unit_count):
    units = unit_count // LANES
    if units == sum(a + b for a, b in CHUNKS):
        return CHUNKS
    return ((2, 0),) + ((3, 1),) * ((units - 2) // 4) + ((1, 0),) * ((units - 2) % 4)


def params():
    return pltpu.CompilerParams(vmem_limit_bytes=64 * 1024 * 1024)


def code_rows(order, grad_out, grad_dither, own_rows, after=()):
    row_count = grad_out.shape[0]
    steps = order.shape[0]
    spec = pl.BlockSpec((row_count, own_rows), lambda i, order: (0, order[i]))

    def body(order_ref, grad_ref, dither_ref, *rest):
        for start in range(0, own_rows, BLOCK):
            grad = grad_ref[:, start : start + BLOCK].astype(jnp.float32)
            top = jnp.max(jnp.abs(grad), axis=1, keepdims=True)
            scale = ((top + EPSILON) / Y_LEVELS).astype(jnp.bfloat16).astype(jnp.float32)
            value = grad + dither_ref[:, start : start + BLOCK] * scale
            rest[-1][0, start : start + BLOCK, :] = value.T.astype(jnp.bfloat16)

    return pl.pallas_call(
        body,
        grid_spec=pltpu.PrefetchScalarGridSpec(
            num_scalar_prefetch=1,
            grid=(steps,),
            in_specs=[spec, spec] + [ANYWHERE] * len(after),
            out_specs=pl.BlockSpec((1, own_rows, row_count), lambda i, order: (i, 0, 0)),
        ),
        out_shape=jax.ShapeDtypeStruct((steps, own_rows, row_count), jnp.bfloat16),
        compiler_params=params(),
        cost_estimate=SMALL_COST,
    )(order, grad_out, grad_dither, *after)


def column_block(rows, start, width):
    return pl.BlockSpec((pl.Element(rows), pl.Element(width)), lambda i, *_: (i * rows, start))


def cut_columns(values, start, width, after=()):
    rows = values.shape[0]
    steps = 4

    def body(in_ref, *rest):
        rest[-1][...] = in_ref[...]

    return pl.pallas_call(
        body,
        grid=(steps,),
        in_specs=[column_block(rows // steps, start, width)] + [ANYWHERE] * len(after),
        out_specs=pl.BlockSpec((rows // steps, width), lambda i: (i, 0)),
        out_shape=jax.ShapeDtypeStruct((rows, width), values.dtype),
        compiler_params=params(),
        cost_estimate=SMALL_COST,
    )(values, *after)


def joined(core, pieces):
    if len(pieces) == 1:
        return pieces[0][0]
    mine, other = (p[0] for p in pieces)
    return jnp.where(
        core == 0, jnp.concatenate([mine, other], axis=1), jnp.concatenate([other, mine], axis=1)
    )


def group_terms(y_block, acts, hidden, feature):
    rows, width = y_block.shape[0], acts.shape[1]
    partial = jnp.dot(y_block, acts, preferred_element_type=jnp.float32)
    column = jnp.broadcast_to(feature, (LANES, rows)).T
    wide = jnp.concatenate([column] * (width // LANES), axis=1)
    out = []
    for start in range(0, rows, BLOCK):
        piece = partial[start : start + BLOCK]
        top = jnp.max(jnp.abs(piece), axis=0, keepdims=True)
        scale = ((top + EPSILON) / W_LEVELS).astype(jnp.bfloat16).astype(jnp.float32)
        out.append(piece + (wide[start : start + BLOCK] + hidden) * scale)
    return jnp.concatenate(out, axis=0)


def held_places(writes):
    first = next(w for w in writes if w is not None)
    places = []
    for w in writes:
        places.append(w if w is not None else (places[-1] if places else first))
    return places


def pair_terms(table, y0, y1, acts, acts0, acts1, dithers0, dithers1, start, widths, ahead, after):
    steps, own_rows = y0[0].shape[:2]
    tokens = acts.shape[0]
    half = steps // 2
    count = len(y0)
    width = sum(widths)
    used = [p for p in range(len(widths)) if widths[p]]
    edges = [sum(widths[:p]) for p in range(len(widths))]

    def body(table_ref, *refs):
        refs = list(refs)
        y0_refs, y1_refs = refs[:count], refs[count : 2 * count]
        a0_ref, a1_ref, h0_ref, h1_ref, f0_ref, f1_ref, acts_ref = refs[2 * count : 2 * count + 7]
        outs = refs[2 * count + 7 + len(after) :]
        step = pl.program_id(0)
        core = table_ref[table.shape[0] - 1]
        if ahead:
            outs[-1][...] = acts_ref[...]
        columns = slice(start, start + width)
        mine = group_terms(joined(core, y0_refs), a0_ref[...], h0_ref[:, columns], f0_ref[...])
        other = group_terms(joined(core, y1_refs), a1_ref[...], h1_ref[:, columns], f1_ref[...])
        total = (mine + other).astype(jnp.bfloat16)
        for at, p in enumerate(used):
            piece = total[:, edges[p] : edges[p] + widths[p]]
            sends = table_ref[(2 + 3 * p) * steps + step]

            @pl.when(sends == 1)
            def _(at=at, piece=piece):
                outs[2 * at][0] = piece

            @pl.when(sends == 0)
            def _(at=at, piece=piece):
                outs[2 * at + 1][0] = piece

    y_specs = [pl.BlockSpec((1, own_rows, y.shape[2]), lambda i, t: (t[i], 0, 0)) for y in y0]
    units = acts.shape[1]
    f_spec = pl.BlockSpec((1, own_rows), lambda i, t: (0, units // own_rows + t[steps + i]))
    a_spec = pl.BlockSpec((tokens, width), lambda i, t: (0, 0))
    h_spec = pl.BlockSpec((1, dithers0.shape[1]), lambda i, t: (0, 0))
    out_specs, out_shape = [], []
    for p in used:
        for side in range(2):
            row = (3 + 3 * p + side) * steps
            out_specs.append(
                pl.BlockSpec((1, own_rows, widths[p]), lambda i, t, row=row: (t[row + i], 0, 0))
            )
            out_shape.append(jax.ShapeDtypeStruct((half, own_rows, widths[p]), jnp.bfloat16))
    ahead_spec = ANYWHERE
    if ahead:
        ahead_spec = column_block(tokens // steps, *ahead)
        out_specs.append(pl.BlockSpec((tokens // steps, ahead[1]), lambda i, t: (i, 0)))
        out_shape.append(jax.ShapeDtypeStruct((tokens, ahead[1]), acts.dtype))
    return pl.pallas_call(
        body,
        grid_spec=pltpu.PrefetchScalarGridSpec(
            num_scalar_prefetch=1,
            grid=(steps,),
            in_specs=[*y_specs, *y_specs, a_spec, a_spec, h_spec, h_spec, f_spec, f_spec]
            + [ahead_spec]
            + [ANYWHERE] * len(after),
            out_specs=out_specs,
        ),
        out_shape=out_shape,
        compiler_params=params(),
        cost_estimate=SMALL_COST,
    )(table, *y0, *y1, acts0, acts1, dithers0, dithers1, dithers0, dithers1, acts, *after)


def add_up(jobs, result, out_shape, after):
    own_rows = out_shape.shape[0]
    steps = own_rows // ADD_ROWS
    in_specs, operands, out_specs, out_shapes, scratch = [], [], [], [], []
    for parts, owners, start in jobs:
        lead = max(owners, 1)
        for arrays, _ in parts:
            for array, width, column in arrays:
                in_specs.append(
                    pl.BlockSpec(
                        (lead, ADD_ROWS, width),
                        lambda i, o=owners, c=column: (1 if o else 0, i, c),
                    )
                )
                operands.append(array)
        if start is None:
            width = sum(w for _, w in parts)
            out_specs.append(pl.BlockSpec((lead, ADD_ROWS, width), lambda i: (0, i, 0)))
            out_shapes.append(jax.ShapeDtypeStruct((lead, own_rows, width), jnp.bfloat16))
    finals = [(sum(w for _, w in parts), start) for parts, _, start in jobs if start is not None]
    aliases = {}
    if finals:
        if result is not None:
            aliases[len(operands) + len(after)] = len(out_shapes)
        out_specs.append(ANYWHERE)
        out_shapes.append(out_shape)
        scratch = [pltpu.VMEM((ADD_ROWS, finals[0][0]), jnp.float32)]
    given = [result] if aliases else []

    def body(*refs):
        refs = list(refs)
        outs = refs[len(operands) + len(after) + len(given) :]
        step = pl.program_id(0)
        at_in = at_out = 0
        for parts, owners, start in jobs:
            edge = 0
            for arrays, width in parts:
                total = refs[at_in][...].astype(jnp.float32)
                for ref in refs[at_in + 1 : at_in + len(arrays)]:
                    total = total + ref[...].astype(jnp.float32)
                at_in += len(arrays)
                if start is None:
                    outs[at_out][:, :, edge : edge + width] = total.astype(jnp.bfloat16)
                else:
                    outs[-1][:, edge : edge + width] = total[0]
                edge += width
            if start is None:
                at_out += 1
            else:
                pltpu.sync_copy(
                    outs[-1], outs[-2].at[pl.ds(step * ADD_ROWS, ADD_ROWS), pl.ds(start, edge)]
                )

    return pl.pallas_call(
        body,
        grid=(steps,),
        in_specs=in_specs + [ANYWHERE] * (len(after) + len(given)),
        out_specs=out_specs,
        out_shape=out_shapes,
        scratch_shapes=scratch,
        input_output_aliases=aliases,
        compiler_params=params(),
        cost_estimate=SMALL_COST,
    )(*operands, *after, *given)


def bits_of(count):
    return [1 << i for i in range(count.bit_length() - 1)]


def relative_order(bits):
    order = [0]
    for bit in reversed(bits):
        order = order + [bit | r for r in order]
    return order


def per_device(grad_out, activations, grad_dither, hidden_dither, feature_dither):
    owners = lax.axis_size("dp")
    feat_width = grad_out.shape[1]
    own_rows = feat_width // owners
    unit_count = activations.shape[1]
    me = lax.axis_index("dp").astype(jnp.int32)
    cores = lax.axis_size("tensor")
    core = lax.axis_index("tensor").astype(jnp.int32)

    def exchange(value, bit):
        return lax.ppermute(value, "dp", [(i, i ^ bit) for i in range(owners)])

    def over_tokens(values):
        if cores == 2:
            return [values, lax.ppermute(values, "tensor", [(0, 1), (1, 0)])]
        return [lax.all_gather(values, "tensor", axis=2, tiled=True)]

    pair_bit, *rest = bits_of(owners)
    part_bits = [rest, [rest[1], rest[0], *rest[2:]]]
    chunks = chunks_of(unit_count)
    widths = [tuple(LANES * c for c in chunk) for chunk in chunks]
    spans, at = [], 0
    for w in widths:
        spans.append((at, sum(w)))
        at += sum(w)

    rel = relative_order(rest)
    rel = rel[len(rel) // 2 :] + rel[: len(rel) // 2]
    rows = [list(range(len(rel)))]
    part_rows = []
    for bits in part_bits:
        within = relative_order(bits[1:])
        place = [within.index(r & ~bits[0]) for r in rel]
        sends = [1 if r & bits[0] else 0 for r in rel]
        part_rows.append(sends)
        for side in (1, 0):
            part_rows.append(held_places([q if s == side else None for q, s in zip(place, sends)]))
    rel_index = jnp.array(rel, jnp.int32)
    table = jnp.concatenate(
        [jnp.array(rows[0], jnp.int32), rel_index ^ me]
        + [jnp.array(r, jnp.int32) for r in part_rows]
        + [core[None]]
    )

    dithers = jnp.concatenate([hidden_dither, feature_dither], axis=1)
    dithers_other = exchange(dithers, pair_bit)
    cuts = {0: cut_columns(activations, *spans[0], after=[dithers])}
    acts_other = {0: exchange(cuts[0], pair_bit)}
    y_send = code_rows(
        rel_index ^ (me ^ pair_bit), grad_out, grad_dither, own_rows, after=[cuts[0], dithers_other]
    )
    y_other = exchange(y_send, pair_bit)
    y_mine = code_rows(rel_index ^ me, grad_out, grad_dither, own_rows, after=[y_send])
    y0 = over_tokens(y_mine)
    cuts[1] = cut_columns(activations, *spans[1], after=[y_mine, acts_other[0], table])
    acts_other[1] = exchange(cuts[1], pair_bit)
    y1 = over_tokens(y_other)

    def terms(chunk, after):
        ahead = spans[chunk + 2] if chunk + 2 < len(spans) else None
        sums = list(pair_terms(
            table, y0, y1, activations, cuts.pop(chunk), acts_other.pop(chunk), dithers, dithers_other,
            spans[chunk][0], widths[chunk], ahead, after,
        ))
        if ahead:
            cuts[chunk + 2] = sums.pop()
        return sums

    stages = len(rest)
    held, sends = {}, {}
    result = None
    out_shape = jax.ShapeDtypeStruct((own_rows, unit_count), jnp.float32)
    made = terms(0, [cuts[1]])
    for step in range(len(spans) + stages - 1):
        arrived = {}
        waits = []
        if step < len(spans):
            used = [p for p in range(2) if widths[step][p]]
            held[step] = {p: [(made[2 * i + 1], widths[step][p], 0)] for i, p in enumerate(used)}
            for i, p in enumerate(used):
                arrived[step, p] = exchange(made[2 * i], part_bits[p][0])
        if step + 2 < len(spans):
            acts_other[step + 2] = exchange(cuts[step + 2], pair_bit)
            waits.append(acts_other[step + 2])
        for key, (send, bit) in sends.items():
            arrived[key] = exchange(send, bit)
        made_before = made
        if step + 1 < len(spans):
            made = terms(step + 1, [s for s, _ in sends.values()] + [made_before[0]])
            waits.append(made[0])
        for (chunk, p), value in arrived.items():
            for q in held[chunk]:
                if p is None or p == q:
                    width = widths[chunk][q]
                    column = 0 if p is not None or q == 0 else widths[chunk][0] // width
                    held[chunk][q].append((value, width, column))
        jobs, keys = [], []
        for chunk in sorted(held):
            stage = step - chunk + 1
            count = len(rel) >> (stage + 1)
            if stage == 1:
                for p, arrays in held[chunk].items():
                    jobs.append(([(arrays, widths[chunk][p])], count, None))
                    keys.append(((chunk, p), part_bits[p][stage]))
            elif count:
                parts = [(arrays, widths[chunk][p]) for p, arrays in held[chunk].items()]
                jobs.append((parts, count, None))
                keys.append(((chunk, None), rest[stage]))
            else:
                parts = [(arrays, widths[chunk][p]) for p, arrays in held[chunk].items()]
                jobs.append((parts, 0, spans[chunk][0]))
        summed = add_up(jobs, result, out_shape, waits)
        if jobs[0][2] is not None:
            result = summed[-1]
            held.pop(min(held))
        sends = {key: (value, bit) for (key, bit), value in zip(keys, summed)}
    return result


def solution(mesh):
    placed = (
        P(("dp", "tensor"), None),
        P("dp", "tensor"),
        P(("dp", "tensor"), None),
        P("dp", "tensor"),
        P("dp", None),
    )
    return jax.shard_map(
        per_device, mesh=mesh, in_specs=placed, out_specs=P("dp", "tensor"), check_vma=False
    )
```

```python
import jax
import jax.numpy as jnp
from jax import lax
from jax.experimental import pallas as pl
from jax.experimental.pallas import tpu as pltpu
from jax.sharding import PartitionSpec as P

BLOCK = 128
Y_LEVELS = 8
W_LEVELS = 7
EPSILON = 1e-06
LANES = 128
LARGE_COST = pl.CostEstimate(flops=2 * 10**11, bytes_accessed=1, transcendentals=0)
SMALL_COST = pl.CostEstimate(flops=1, bytes_accessed=1, transcendentals=0)
ANYWHERE = pl.BlockSpec(memory_space=pl.ANY)

CHUNKS = (4, 8, 8, 8, 8, 8, 8, 4)


def chunks_of(unit_count):
    units = unit_count // LANES
    if units == sum(CHUNKS):
        return CHUNKS
    return (2,) + (4,) * ((units - 2) // 4) + (1,) * ((units - 2) % 4)


def params():
    return pltpu.CompilerParams(vmem_limit_bytes=64 * 1024 * 1024)


def code_rows(order, grad_out, grad_dither, own_rows, after=()):
    row_count = grad_out.shape[0]
    steps = order.shape[0]
    spec = pl.BlockSpec((row_count, own_rows), lambda i, order: (0, order[i]))

    def body(order_ref, grad_ref, dither_ref, *rest):
        for start in range(0, own_rows, BLOCK):
            grad = grad_ref[:, start : start + BLOCK].astype(jnp.float32)
            top = jnp.max(jnp.abs(grad), axis=1, keepdims=True)
            scale = ((top + EPSILON) / Y_LEVELS).astype(jnp.bfloat16).astype(jnp.float32)
            value = grad + dither_ref[:, start : start + BLOCK] * scale
            rest[-1][0, start : start + BLOCK, :] = value.T.astype(jnp.bfloat16)

    return pl.pallas_call(
        body,
        grid_spec=pltpu.PrefetchScalarGridSpec(
            num_scalar_prefetch=1,
            grid=(steps,),
            in_specs=[spec, spec] + [ANYWHERE] * len(after),
            out_specs=pl.BlockSpec((1, own_rows, row_count), lambda i, order: (i, 0, 0)),
        ),
        out_shape=jax.ShapeDtypeStruct((steps, own_rows, row_count), jnp.bfloat16),
        compiler_params=params(),
        cost_estimate=SMALL_COST,
    )(order, grad_out, grad_dither, *after)


def column_block(rows, start, width):
    return pl.BlockSpec((pl.Element(rows), pl.Element(width)), lambda i, *_: (i * rows, start))


def cut_columns(values, start, width, after=()):
    rows = values.shape[0]
    steps = 4

    def body(in_ref, *rest):
        rest[-1][...] = in_ref[...]

    return pl.pallas_call(
        body,
        grid=(steps,),
        in_specs=[column_block(rows // steps, start, width)] + [ANYWHERE] * len(after),
        out_specs=pl.BlockSpec((rows // steps, width), lambda i: (i, 0)),
        out_shape=jax.ShapeDtypeStruct((rows, width), values.dtype),
        compiler_params=params(),
        cost_estimate=SMALL_COST,
    )(values, *after)


def joined(core, pieces):
    if len(pieces) == 1:
        return pieces[0][0]
    mine, other = (p[0] for p in pieces)
    return jnp.where(
        core == 0, jnp.concatenate([mine, other], axis=1), jnp.concatenate([other, mine], axis=1)
    )


def group_terms(y_block, acts, hidden, feature):
    rows, width = y_block.shape[0], acts.shape[1]
    partial = jnp.dot(y_block, acts, preferred_element_type=jnp.float32)
    column = jnp.broadcast_to(feature, (LANES, rows)).T
    wide = jnp.concatenate([column] * (width // LANES), axis=1)
    out = []
    for start in range(0, rows, BLOCK):
        piece = partial[start : start + BLOCK]
        top = jnp.max(jnp.abs(piece), axis=0, keepdims=True)
        scale = ((top + EPSILON) / W_LEVELS).astype(jnp.bfloat16).astype(jnp.float32)
        out.append(piece + (wide[start : start + BLOCK] + hidden) * scale)
    return jnp.concatenate(out, axis=0)


def pair_terms(owner, core, y0, y1, acts, acts0, acts1, dithers0, dithers1, start, ahead, after):
    steps, own_rows = y0[0].shape[:2]
    tokens, units = acts.shape
    count = len(y0)
    width = acts0.shape[1]

    def body(table_ref, *refs):
        refs = list(refs)
        y0_refs, y1_refs = refs[:count], refs[count : 2 * count]
        a0_ref, a1_ref, h0_ref, h1_ref, f0_ref, f1_ref, acts_ref = refs[2 * count : 2 * count + 7]
        outs = refs[2 * count + 7 + len(after) :]
        core = table_ref[steps]
        if ahead:
            outs[1][...] = acts_ref[...]
        columns = slice(start, start + width)
        mine = group_terms(joined(core, y0_refs), a0_ref[...], h0_ref[:, columns], f0_ref[...])
        other = group_terms(joined(core, y1_refs), a1_ref[...], h1_ref[:, columns], f1_ref[...])
        outs[0][...] = (mine + other).astype(jnp.bfloat16)

    y_specs = [pl.BlockSpec((1, own_rows, y.shape[2]), lambda i, t: (i, 0, 0)) for y in y0]
    f_spec = pl.BlockSpec((1, own_rows), lambda i, t: (0, units // own_rows + t[i]))
    a_spec = pl.BlockSpec((tokens, width), lambda i, t: (0, 0))
    h_spec = pl.BlockSpec((1, dithers0.shape[1]), lambda i, t: (0, 0))
    out_specs = [pl.BlockSpec((own_rows, width), lambda i, t: (i, 0))]
    out_shape = [jax.ShapeDtypeStruct((steps * own_rows, width), jnp.bfloat16)]
    ahead_spec = ANYWHERE
    if ahead:
        ahead_spec = column_block(tokens // steps, *ahead)
        out_specs.append(pl.BlockSpec((tokens // steps, ahead[1]), lambda i, t: (i, 0)))
        out_shape.append(jax.ShapeDtypeStruct((tokens, ahead[1]), acts.dtype))
    return pl.pallas_call(
        body,
        grid_spec=pltpu.PrefetchScalarGridSpec(
            num_scalar_prefetch=1,
            grid=(steps,),
            in_specs=[*y_specs, *y_specs, a_spec, a_spec, h_spec, h_spec, f_spec, f_spec]
            + [ahead_spec]
            + [ANYWHERE] * len(after),
            out_specs=out_specs,
        ),
        out_shape=out_shape,
        compiler_params=params(),
        cost_estimate=LARGE_COST,
    )(
        jnp.concatenate([owner, core[None]]),
        *y0, *y1, acts0, acts1, dithers0, dithers1, dithers0, dithers1, acts, *after,
    )


def finish(summed, result, out_shape, start):
    own_rows, width = summed.shape
    given = [] if result is None else [result]

    def body(sum_ref, *rest):
        out_ref, held, sem = rest[-3:]
        held[...] = sum_ref[...].astype(jnp.float32)
        copy = pltpu.make_async_copy(held, out_ref.at[:, pl.ds(start, width)], sem)
        copy.start()
        copy.wait()

    return pl.pallas_call(
        body,
        in_specs=[pl.BlockSpec(memory_space=pltpu.VMEM)] + [ANYWHERE] * len(given),
        out_specs=ANYWHERE,
        out_shape=out_shape,
        scratch_shapes=[pltpu.VMEM((own_rows, width), jnp.float32), pltpu.SemaphoreType.DMA],
        input_output_aliases={1: 0} if given else {},
        compiler_params=params(),
        cost_estimate=SMALL_COST,
    )(summed, *given)


def per_device(grad_out, activations, grad_dither, hidden_dither, feature_dither):
    owners = lax.axis_size("dp")
    own_rows = grad_out.shape[1] // owners
    unit_count = activations.shape[1]
    me = lax.axis_index("dp").astype(jnp.int32)
    cores = lax.axis_size("tensor")
    core = lax.axis_index("tensor").astype(jnp.int32)
    sides = [[i for i in range(owners) if i % 2 == side] for side in range(2)]

    def exchange(value):
        return lax.ppermute(value, "dp", [(i, i ^ 1) for i in range(owners)])

    def over_tokens(values):
        if cores == 2:
            return [values, lax.ppermute(values, "tensor", [(0, 1), (1, 0)])]
        return [lax.all_gather(values, "tensor", axis=2, tiled=True)]

    spans, at = [], 0
    for c in chunks_of(unit_count):
        spans.append((at, c * LANES))
        at += c * LANES

    owner = 2 * jnp.arange(owners // 2, dtype=jnp.int32) + me % 2
    dithers = jnp.concatenate([hidden_dither, feature_dither], axis=1)
    dithers_other = exchange(dithers)
    cuts = {0: cut_columns(activations, *spans[0], after=[dithers])}
    acts_other = {0: exchange(cuts[0])}
    y_send = code_rows(owner ^ 1, grad_out, grad_dither, own_rows, after=[cuts[0], dithers_other])
    y_other = exchange(y_send)
    y_mine = code_rows(owner, grad_out, grad_dither, own_rows, after=[y_send])
    y0 = over_tokens(y_mine)
    cuts[1] = cut_columns(activations, *spans[1], after=[y_mine, acts_other[0]])
    acts_other[1] = exchange(cuts[1])
    y1 = over_tokens(y_other)

    result = None
    out_shape = jax.ShapeDtypeStruct((own_rows, unit_count), jnp.float32)
    after = [cuts[1]]
    waiting = []
    for chunk, (start, width) in enumerate(spans):
        ahead = spans[chunk + 2] if chunk + 2 < len(spans) else None
        terms, *cut = pair_terms(
            owner, core, y0, y1, activations, cuts.pop(chunk), acts_other.pop(chunk),
            dithers, dithers_other, start, ahead, after,
        )
        if ahead:
            cuts[chunk + 2] = cut[0]
            acts_other[chunk + 2] = exchange(cut[0])
        after = [terms]
        waiting.append((lax.psum_scatter(
            terms, "dp", scatter_dimension=0, axis_index_groups=sides, tiled=True
        ), start))
    for summed, start in waiting:
        result = finish(summed, result, out_shape, start)
    return result


def solution(mesh):
    placed = (
        P(("dp", "tensor"), None),
        P("dp", "tensor"),
        P(("dp", "tensor"), None),
        P("dp", "tensor"),
        P("dp", None),
    )
    return jax.shard_map(
        per_device, mesh=mesh, in_specs=placed, out_specs=P("dp", "tensor"), check_vma=False
    )
```

```python
import jax
import jax.numpy as jnp
from jax import lax
from jax.experimental import pallas as pl
from jax.experimental.pallas import tpu as pltpu
from jax.sharding import PartitionSpec as P

BLOCK = 128
Y_LEVELS = 8
W_LEVELS = 7
EPSILON = 1e-06
LANES = 128
LARGE_COST = pl.CostEstimate(flops=2 * 10**11, bytes_accessed=1, transcendentals=0)
SMALL_COST = pl.CostEstimate(flops=1, bytes_accessed=1, transcendentals=0)
ANYWHERE = pl.BlockSpec(memory_space=pl.ANY)

CHUNKS = ((4, 4), (8, 8), (8, 8), (6, 6), (2, 2))


def chunks_of(unit_count):
    units = unit_count // LANES
    if units == sum(a + b for a, b in CHUNKS):
        return CHUNKS
    count = (units - 2) // 6
    last = (units - 2 - 6 * count) // 2
    return ((1, 1),) + ((3, 3),) * count + (((last, last),) if last else ())


def params():
    return pltpu.CompilerParams(vmem_limit_bytes=64 * 1024 * 1024)


def code_rows(order, grad_out, grad_dither, own_rows, after=()):
    row_count = grad_out.shape[0]
    steps = order.shape[0]
    spec = pl.BlockSpec((row_count, own_rows), lambda i, order: (0, order[i]))

    def body(order_ref, grad_ref, dither_ref, *rest):
        for start in range(0, own_rows, BLOCK):
            grad = grad_ref[:, start : start + BLOCK].astype(jnp.float32)
            top = jnp.max(jnp.abs(grad), axis=1, keepdims=True)
            scale = ((top + EPSILON) / Y_LEVELS).astype(jnp.bfloat16).astype(jnp.float32)
            value = grad + dither_ref[:, start : start + BLOCK] * scale
            rest[-1][0, start : start + BLOCK, :] = value.astype(jnp.bfloat16).T

    return pl.pallas_call(
        body,
        grid_spec=pltpu.PrefetchScalarGridSpec(
            num_scalar_prefetch=1,
            grid=(steps,),
            in_specs=[spec, spec] + [ANYWHERE] * len(after),
            out_specs=pl.BlockSpec((1, own_rows, row_count), lambda i, order: (i, 0, 0)),
        ),
        out_shape=jax.ShapeDtypeStruct((steps, own_rows, row_count), jnp.bfloat16),
        compiler_params=params(),
        cost_estimate=SMALL_COST,
    )(order, grad_out, grad_dither, *after)


def column_block(rows, start, width):
    return pl.BlockSpec((pl.Element(rows), pl.Element(width)), lambda i, *_: (i * rows, start))


def cut_columns(values, start, width, after=()):
    rows = values.shape[0]
    steps = 4

    def body(in_ref, *rest):
        rest[-1][...] = in_ref[...]

    return pl.pallas_call(
        body,
        grid=(steps,),
        in_specs=[column_block(rows // steps, start, width)] + [ANYWHERE] * len(after),
        out_specs=pl.BlockSpec((rows // steps, width), lambda i: (i, 0)),
        out_shape=jax.ShapeDtypeStruct((rows, width), values.dtype),
        compiler_params=params(),
        cost_estimate=SMALL_COST,
    )(values, *after)


def joined(core, pieces):
    if len(pieces) == 1:
        return pieces[0][0]
    mine, other = (p[0] for p in pieces)
    return jnp.where(
        core == 0, jnp.concatenate([mine, other], axis=1), jnp.concatenate([other, mine], axis=1)
    )


def group_terms(y_block, acts, hidden, feature):
    rows, width = y_block.shape[0], acts.shape[1]
    partial = jnp.dot(y_block, acts, preferred_element_type=jnp.float32)
    column = jnp.broadcast_to(feature, (LANES, rows)).T
    wide = jnp.concatenate([column] * (width // LANES), axis=1)
    out = []
    for start in range(0, rows, BLOCK):
        piece = partial[start : start + BLOCK]
        top = jnp.max(jnp.abs(piece), axis=0, keepdims=True)
        scale = ((top + EPSILON) / W_LEVELS).astype(jnp.bfloat16).astype(jnp.float32)
        out.append(piece + (wide[start : start + BLOCK] + hidden) * scale)
    return jnp.concatenate(out, axis=0)


def pair_terms(owner, core, y0, y1, acts, acts0, acts1, dithers0, dithers1, start, ahead, after):
    steps, own_rows = y0[0].shape[:2]
    tokens, units = acts.shape
    half = steps // 2
    count, both = len(y0), len(y0) + len(y1)
    width = acts0.shape[1]

    def body(table_ref, *refs):
        refs = list(refs)
        y0_refs, y1_refs = refs[:count], refs[count : both]
        a0_ref, a1_ref, h0_ref, h1_ref, f0_ref, f1_ref, acts_ref = refs[both : both + 7]
        outs = refs[both + 7 + len(after) :]
        core = table_ref[steps]
        if ahead:
            outs[2][...] = acts_ref[...]
        columns = slice(start, start + width)
        mine = group_terms(joined(core, y0_refs), a0_ref[...], h0_ref[:, columns], f0_ref[...])
        other = group_terms(joined(core, y1_refs), a1_ref[...], h1_ref[:, columns], f1_ref[...])
        total = (mine + other).astype(jnp.bfloat16)
        step = pl.program_id(0)

        @pl.when(step < half)
        def _():
            outs[0][...] = total

        @pl.when(step >= half)
        def _():
            outs[1][...] = total


    y0_specs, y1_specs = (
        [pl.BlockSpec((1, own_rows, y.shape[2]), lambda i, t: (i, 0, 0)) for y in ys] for ys in (y0, y1)
    )
    f_spec = pl.BlockSpec((1, own_rows), lambda i, t: (0, units // own_rows + t[i]))
    a_spec = pl.BlockSpec((tokens, width), lambda i, t: (0, 0))
    h_spec = pl.BlockSpec((1, dithers0.shape[1]), lambda i, t: (0, 0))
    out_specs = [
        pl.BlockSpec((own_rows, width), lambda i, t: (jnp.minimum(i, half - 1), 0)),
        pl.BlockSpec((own_rows, width), lambda i, t: (jnp.maximum(i - half, 0), 0)),
    ]
    out_shape = [jax.ShapeDtypeStruct((half * own_rows, width), jnp.bfloat16)] * 2
    ahead_spec = ANYWHERE
    if ahead:
        ahead_spec = column_block(tokens // steps, *ahead)
        out_specs.append(pl.BlockSpec((tokens // steps, ahead[1]), lambda i, t: (i, 0)))
        out_shape.append(jax.ShapeDtypeStruct((tokens, ahead[1]), acts.dtype))
    return pl.pallas_call(
        body,
        grid_spec=pltpu.PrefetchScalarGridSpec(
            num_scalar_prefetch=1,
            grid=(steps,),
            in_specs=[*y0_specs, *y1_specs, a_spec, a_spec, h_spec, h_spec, f_spec, f_spec]
            + [ahead_spec]
            + [ANYWHERE] * len(after),
            out_specs=out_specs,
        ),
        out_shape=out_shape,
        compiler_params=params(),
        cost_estimate=LARGE_COST,
    )(
        jnp.concatenate([owner, core[None]]),
        *y0, *y1, acts0, acts1, dithers0, dithers1, dithers0, dithers1, acts, *after,
    )


def add_up(keeps, comes, after):
    rows = keeps[0].shape[0]
    widths = [k.shape[1] for k in keeps]
    step_rows = LANES

    def body(*refs):
        out_ref = refs[-1]
        edge = 0
        for at, width in enumerate(widths):
            total = refs[2 * at][...].astype(jnp.float32) + refs[2 * at + 1][...].astype(jnp.float32)
            out_ref[:, edge : edge + width] = total.astype(jnp.bfloat16)
            edge += width

    operands = [v for pair in zip(keeps, comes) for v in pair]
    return pl.pallas_call(
        body,
        grid=(rows // step_rows,),
        in_specs=[pl.BlockSpec((step_rows, v.shape[1]), lambda i: (i, 0)) for v in operands]
        + [ANYWHERE] * len(after),
        out_specs=pl.BlockSpec((step_rows, sum(widths)), lambda i: (i, 0)),
        out_shape=jax.ShapeDtypeStruct((rows, sum(widths)), jnp.bfloat16),
        compiler_params=params(),
        cost_estimate=SMALL_COST,
    )(*operands, *after)


def finish(summed, result, out_shape, start):
    own_rows, width = summed.shape
    given = [] if result is None else [result]

    def body(sum_ref, *rest):
        out_ref, held, sem = rest[-3:]
        held[...] = sum_ref[...].astype(jnp.float32)
        copy = pltpu.make_async_copy(held, out_ref.at[:, pl.ds(start, width)], sem)
        copy.start()
        copy.wait()

    return pl.pallas_call(
        body,
        in_specs=[pl.BlockSpec(memory_space=pltpu.VMEM)] + [ANYWHERE] * len(given),
        out_specs=ANYWHERE,
        out_shape=out_shape,
        scratch_shapes=[pltpu.VMEM((own_rows, width), jnp.float32), pltpu.SemaphoreType.DMA],
        input_output_aliases={1: 0} if given else {},
        compiler_params=params(),
        cost_estimate=SMALL_COST,
    )(summed, *given)


def per_device(grad_out, activations, grad_dither, hidden_dither, feature_dither):
    owners = lax.axis_size("dp")
    own_rows = grad_out.shape[1] // owners
    unit_count = activations.shape[1]
    me = lax.axis_index("dp").astype(jnp.int32)
    cores = lax.axis_size("tensor")
    core = lax.axis_index("tensor").astype(jnp.int32)
    pair_bits = (1, 2)
    lines = [[i for i in range(owners) if i % 4 == r] for r in range(4)]

    def exchange(value, bit):
        return lax.ppermute(value, "dp", [(i, i ^ bit) for i in range(owners)])

    def over_tokens(values, early):
        if cores == 2 and not early:
            return [values, lax.ppermute(values, "tensor", [(0, 1), (1, 0)])]
        return [lax.all_gather(values, "tensor", axis=2, tiled=True)]

    steps = chunks_of(unit_count)
    spans, at = [], 0
    for chunk in steps:
        spans.append([])
        for c in chunk:
            spans[-1].append((at, c * LANES))
            at += c * LANES

    line = 4 * jnp.arange(owners // 4, dtype=jnp.int32)
    owner = []
    for part in range(2):
        mine = line + me % 4
        owner.append(jnp.concatenate([mine ^ pair_bits[1 - part], mine]))

    dithers = jnp.concatenate([hidden_dither, feature_dither], axis=1)
    dithers_other = [exchange(dithers, bit) for bit in pair_bits]
    cuts, acts_other, y0, y1 = {}, {}, [], []
    after = [dithers]
    for part, bit in enumerate(pair_bits):
        cuts[0, part] = cut_columns(activations, *spans[0][part], after=after)
        acts_other[0, part] = exchange(cuts[0, part], bit)
        after = [cuts[0, part]]
    after = after + dithers_other
    y_other = []
    for part, bit in enumerate(pair_bits):
        y_send = code_rows(owner[part] ^ bit, grad_out, grad_dither, own_rows, after=after)
        y_other.append(exchange(y_send, bit))
        after = [y_send]
    for part in range(2):
        y_mine = code_rows(owner[part], grad_out, grad_dither, own_rows, after=after)
        y0.append(over_tokens(y_mine, True))
        after = [y_mine]
    for part, bit in enumerate(pair_bits):
        cuts[1, part] = cut_columns(activations, *spans[1][part], after=after + [acts_other[0, part]])
        acts_other[1, part] = exchange(cuts[1, part], bit)
        after = [cuts[1, part]]
    y1 = [over_tokens(y, False) for y in y_other]

    result = None
    out_shape = jax.ShapeDtypeStruct((own_rows, unit_count), jnp.float32)
    waiting, keeps, comes = [], None, None
    for step, chunk in enumerate(spans):
        keeps_now, comes_now = [], []
        for part, (start, width) in enumerate(chunk):
            ahead = spans[step + 2][part] if step + 2 < len(spans) else None
            send, keep, *cut = pair_terms(
                owner[part], core, y0[part], y1[part], activations, cuts.pop((step, part)),
                acts_other.pop((step, part)), dithers, dithers_other[part], start, ahead, after,
            )
            if ahead:
                cuts[step + 2, part] = cut[0]
                acts_other[step + 2, part] = exchange(cut[0], pair_bits[part])
            keeps_now.append(keep)
            comes_now.append(exchange(send, pair_bits[1 - part]))
            after = [send]
        if step:
            waiting.append(add_up(keeps, comes, after))
            after = [waiting[-1]]
        keeps, comes = keeps_now, comes_now
    waiting.append(add_up(keeps, comes, after))
    for chunk, terms in zip(spans, waiting):
        summed = lax.psum_scatter(
            terms, "dp", scatter_dimension=0, axis_index_groups=lines, tiled=True
        )
        result = finish(summed, result, out_shape, chunk[0][0])
    return result


def solution(mesh):
    placed = (
        P(("dp", "tensor"), None),
        P("dp", "tensor"),
        P(("dp", "tensor"), None),
        P("dp", "tensor"),
        P("dp", None),
    )
    return jax.shard_map(
        per_device, mesh=mesh, in_specs=placed, out_specs=P("dp", "tensor"), check_vma=False
    )
```

```python
import jax
import jax.numpy as jnp
from jax import lax
from jax.experimental import pallas as pl
from jax.experimental.pallas import tpu as pltpu
from jax.sharding import PartitionSpec as P

BLOCK = 128
Y_LEVELS = 8
W_LEVELS = 7
EPSILON = 1e-06
LANES = 128
LARGE_COST = pl.CostEstimate(flops=2 * 10**11, bytes_accessed=1, transcendentals=0)
SMALL_COST = pl.CostEstimate(flops=1, bytes_accessed=1, transcendentals=0)
ANYWHERE = pl.BlockSpec(memory_space=pl.ANY)

CHUNKS = ((3, 3), (5, 5), (8, 8), (8, 8), (4, 4))


def chunks_of(unit_count):
    units = unit_count // LANES
    if units == sum(a + b for a, b in CHUNKS):
        return CHUNKS
    count = (units - 2) // 6
    last = (units - 2 - 6 * count) // 2
    return ((1, 1),) + ((3, 3),) * count + (((last, last),) if last else ())


def params():
    return pltpu.CompilerParams(vmem_limit_bytes=64 * 1024 * 1024)


def code_rows(order, grad_out, grad_dither, own_rows, after=()):
    row_count = grad_out.shape[0]
    steps = order.shape[0]
    spec = pl.BlockSpec((row_count, own_rows), lambda i, order: (0, order[i]))

    def body(order_ref, grad_ref, dither_ref, *rest):
        for start in range(0, own_rows, BLOCK):
            grad = grad_ref[:, start : start + BLOCK].astype(jnp.float32)
            top = jnp.max(jnp.abs(grad), axis=1, keepdims=True)
            scale = ((top + EPSILON) / Y_LEVELS).astype(jnp.bfloat16).astype(jnp.float32)
            value = grad + dither_ref[:, start : start + BLOCK] * scale
            rest[-1][0, start : start + BLOCK, :] = value.astype(jnp.bfloat16).T

    return pl.pallas_call(
        body,
        grid_spec=pltpu.PrefetchScalarGridSpec(
            num_scalar_prefetch=1,
            grid=(steps,),
            in_specs=[spec, spec] + [ANYWHERE] * len(after),
            out_specs=pl.BlockSpec((1, own_rows, row_count), lambda i, order: (i, 0, 0)),
        ),
        out_shape=jax.ShapeDtypeStruct((steps, own_rows, row_count), jnp.bfloat16),
        compiler_params=params(),
        cost_estimate=SMALL_COST,
    )(order, grad_out, grad_dither, *after)


def column_block(rows, start, width):
    return pl.BlockSpec((pl.Element(rows), pl.Element(width)), lambda i, *_: (i * rows, start))


def cut_columns(values, spans, after=()):
    rows = values.shape[0]
    steps = 4

    def body(*refs):
        for in_ref, out_ref in zip(refs, refs[-len(spans) :]):
            out_ref[...] = in_ref[...]

    return pl.pallas_call(
        body,
        grid=(steps,),
        in_specs=[column_block(rows // steps, *span) for span in spans] + [ANYWHERE] * len(after),
        out_specs=[pl.BlockSpec((rows // steps, width), lambda i: (i, 0)) for _, width in spans],
        out_shape=[jax.ShapeDtypeStruct((rows, width), values.dtype) for _, width in spans],
        compiler_params=params(),
        cost_estimate=SMALL_COST,
    )(*[values] * len(spans), *after)


def joined(core, pieces):
    if len(pieces) == 1:
        return pieces[0][0]
    mine, other = (p[0] for p in pieces)
    return jnp.where(
        core == 0, jnp.concatenate([mine, other], axis=1), jnp.concatenate([other, mine], axis=1)
    )


def group_terms(y_block, acts, hidden, feature):
    rows, width = y_block.shape[0], acts.shape[1]
    partial = jnp.dot(y_block, acts, preferred_element_type=jnp.float32)
    column = jnp.broadcast_to(feature, (LANES, rows)).T
    wide = jnp.concatenate([column] * (width // LANES), axis=1)
    out = []
    for start in range(0, rows, BLOCK):
        piece = partial[start : start + BLOCK]
        top = jnp.max(jnp.abs(piece), axis=0, keepdims=True)
        scale = ((top + EPSILON) / W_LEVELS).astype(jnp.bfloat16).astype(jnp.float32)
        out.append(piece + (wide[start : start + BLOCK] + hidden) * scale)
    return jnp.concatenate(out, axis=0)


def pair_terms(owner, rank, core, y0, y1, acts, acts0, acts1, dithers, start, ahead, after):
    steps, own_rows = y0[0].shape[:2]
    tokens, units = acts.shape
    half = steps // 2
    count, both = len(y0), len(y0) + len(y1)
    width = acts0.shape[1]

    def body(table_ref, *refs):
        refs = list(refs)
        y0_refs, y1_refs = refs[:count], refs[count : both]
        a0_ref, a1_ref, h0_ref, h1_ref, f0_ref, f1_ref = refs[both : both + 6]
        cut_refs = refs[both + 6 : both + 6 + len(ahead)]
        outs = refs[both + 6 + len(ahead) + len(after) :]
        core = table_ref[steps + 2]
        for cut_ref, out_ref in zip(cut_refs, outs[2:]):
            out_ref[...] = cut_ref[...]
        columns = slice(start, start + width)
        mine = group_terms(joined(core, y0_refs), a0_ref[...], h0_ref[0, :, columns], f0_ref[0])
        other = group_terms(joined(core, y1_refs), a1_ref[...], h1_ref[0, :, columns], f1_ref[0])
        total = (mine + other).astype(jnp.bfloat16)
        step = pl.program_id(0)

        @pl.when(step < half)
        def _():
            outs[0][...] = total

        @pl.when(step >= half)
        def _():
            outs[1][...] = total


    y0_specs, y1_specs = (
        [pl.BlockSpec((1, own_rows, y.shape[2]), lambda i, t: (i, 0, 0)) for y in ys] for ys in (y0, y1)
    )
    f_specs = [
        pl.BlockSpec((1, 1, own_rows), lambda i, t, g=g: (t[steps + g], 0, units // own_rows + t[i]))
        for g in range(2)
    ]
    h_specs = [
        pl.BlockSpec((1, 1, dithers.shape[2]), lambda i, t, g=g: (t[steps + g], 0, 0))
        for g in range(2)
    ]
    a_spec = pl.BlockSpec((tokens, width), lambda i, t: (0, 0))
    out_specs = [
        pl.BlockSpec((own_rows, width), lambda i, t: (jnp.minimum(i, half - 1), 0)),
        pl.BlockSpec((own_rows, width), lambda i, t: (jnp.maximum(i - half, 0), 0)),
    ]
    out_shape = [jax.ShapeDtypeStruct((half * own_rows, width), jnp.bfloat16)] * 2
    for _, cut_width in ahead:
        out_specs.append(pl.BlockSpec((tokens // steps, cut_width), lambda i, t: (i, 0)))
        out_shape.append(jax.ShapeDtypeStruct((tokens, cut_width), acts.dtype))
    return pl.pallas_call(
        body,
        grid_spec=pltpu.PrefetchScalarGridSpec(
            num_scalar_prefetch=1,
            grid=(steps,),
            in_specs=[*y0_specs, *y1_specs, a_spec, a_spec, *h_specs, *f_specs]
            + [column_block(tokens // steps, *span) for span in ahead]
            + [ANYWHERE] * len(after),
            out_specs=out_specs,
        ),
        out_shape=out_shape,
        compiler_params=params(),
        cost_estimate=LARGE_COST,
    )(
        jnp.concatenate([owner, rank, core[None]]),
        *y0, *y1, acts0, acts1, *[dithers] * 4, *[acts] * len(ahead), *after,
    )


def add_up(keeps, comes, after):
    rows = keeps[0].shape[0]
    widths = [k.shape[1] for k in keeps]
    step_rows = LANES

    def body(*refs):
        out_ref = refs[-1]
        edge = 0
        for at, width in enumerate(widths):
            total = refs[2 * at][...].astype(jnp.float32) + refs[2 * at + 1][...].astype(jnp.float32)
            out_ref[:, edge : edge + width] = total.astype(jnp.bfloat16)
            edge += width

    operands = [v for pair in zip(keeps, comes) for v in pair]
    return pl.pallas_call(
        body,
        grid=(rows // step_rows,),
        in_specs=[pl.BlockSpec((step_rows, v.shape[1]), lambda i: (i, 0)) for v in operands]
        + [ANYWHERE] * len(after),
        out_specs=pl.BlockSpec((step_rows, sum(widths)), lambda i: (i, 0)),
        out_shape=jax.ShapeDtypeStruct((rows, sum(widths)), jnp.bfloat16),
        compiler_params=params(),
        cost_estimate=SMALL_COST,
    )(*operands, *after)


def finish(summed, result, out_shape, start):
    own_rows, width = summed.shape
    given = [] if result is None else [result]

    def body(sum_ref, *rest):
        out_ref, held, sem = rest[-3:]
        held[...] = sum_ref[...].astype(jnp.float32)
        copy = pltpu.make_async_copy(held, out_ref.at[:, pl.ds(start, width)], sem)
        copy.start()
        copy.wait()

    return pl.pallas_call(
        body,
        in_specs=[pl.BlockSpec(memory_space=pltpu.VMEM)] + [ANYWHERE] * len(given),
        out_specs=ANYWHERE,
        out_shape=out_shape,
        scratch_shapes=[pltpu.VMEM((own_rows, width), jnp.float32), pltpu.SemaphoreType.DMA],
        input_output_aliases={1: 0} if given else {},
        compiler_params=params(),
        cost_estimate=SMALL_COST,
    )(summed, *given)


def per_device(grad_out, activations, grad_dither, hidden_dither, feature_dither):
    owners = lax.axis_size("dp")
    own_rows = grad_out.shape[1] // owners
    unit_count = activations.shape[1]
    me = lax.axis_index("dp").astype(jnp.int32)
    cores = lax.axis_size("tensor")
    core = lax.axis_index("tensor").astype(jnp.int32)
    pair_bits = (1, 2)
    lines = [[i for i in range(owners) if i % 4 == r] for r in range(4)]

    def exchange(value, bit):
        return lax.ppermute(value, "dp", [(i, i ^ bit) for i in range(owners)])

    def over_tokens(values):
        if cores == 2:
            return [values, lax.ppermute(values, "tensor", [(0, 1), (1, 0)])]
        return [lax.all_gather(values, "tensor", axis=2, tiled=True)]

    steps = chunks_of(unit_count)
    spans, at = [], 0
    for chunk in steps:
        spans.append([])
        for c in chunk:
            spans[-1].append((at, c * LANES))
            at += c * LANES

    line = 4 * jnp.arange(owners // 4, dtype=jnp.int32)
    owner = []
    for part in range(2):
        mine = line + me % 4
        owner.append(jnp.concatenate([mine ^ pair_bits[1 - part], mine]))

    quads = [list(range(i, i + 4)) for i in range(0, owners, 4)]
    dithers = lax.all_gather(
        jnp.concatenate([hidden_dither, feature_dither], axis=1), "dp", axis_index_groups=quads
    )
    y_other, y0, after = [], [], []
    for part, bit in enumerate(pair_bits):
        y_send = code_rows(owner[part] ^ bit, grad_out, grad_dither, own_rows, after)
        y_other.append(exchange(y_send, bit))
        after = [y_send]
    first = cut_columns(activations, [*spans[0], *spans[1]], after)
    cuts = {(at // 2, at % 2): values for at, values in enumerate(first)}
    acts_other = {key: exchange(values, pair_bits[key[1]]) for key, values in cuts.items()}
    after = [first[0], dithers]
    for part in range(2):
        y_mine = code_rows(owner[part], grad_out, grad_dither, own_rows, after)
        y0.append(over_tokens(y_mine))
        after = [y_mine]
    after = [y_mine, y_other[1], acts_other[0, 1]]
    y1 = [over_tokens(y) for y in y_other]

    result = None
    out_shape = jax.ShapeDtypeStruct((own_rows, unit_count), jnp.float32)
    waiting, keeps, comes = [], None, None
    for step, chunk in enumerate(spans):
        keeps_now, comes_now = [], []
        for part, (start, width) in enumerate(chunk):
            if step == 1 and part == 1:
                waiting.append(add_up(keeps, comes, after))
                after = [waiting[-1]]
            ahead = spans[step + 2] if part and step + 2 < len(spans) else []
            rank = jnp.stack([me % 4, me % 4 ^ pair_bits[part]])
            send, keep, *cut = pair_terms(
                owner[part], rank, core, y0[part], y1[part], activations, cuts.pop((step, part)),
                acts_other.pop((step, part)), dithers, start, ahead, after,
            )
            for p, columns in enumerate(cut):
                cuts[step + 2, p] = columns
                acts_other[step + 2, p] = exchange(columns, pair_bits[p])
            keeps_now.append(keep)
            comes_now.append(exchange(send, pair_bits[1 - part]))
            after = [send]
        if step > 1:
            waiting.append(add_up(keeps, comes, after))
            after = [waiting[-1]]
        keeps, comes = keeps_now, comes_now
    waiting.append(add_up(keeps, comes, after))
    for chunk, terms in zip(spans, waiting):
        summed = lax.psum_scatter(
            terms, "dp", scatter_dimension=0, axis_index_groups=lines, tiled=True
        )
        result = finish(summed, result, out_shape, chunk[0][0])
    return result


def solution(mesh):
    placed = (
        P(("dp", "tensor"), None),
        P("dp", "tensor"),
        P(("dp", "tensor"), None),
        P("dp", "tensor"),
        P("dp", None),
    )
    return jax.shard_map(
        per_device, mesh=mesh, in_specs=placed, out_specs=P("dp", "tensor"), check_vma=False
    )
```

```python
import jax
import jax.numpy as jnp
from jax import lax
from jax.experimental import pallas as pl
from jax.experimental.pallas import tpu as pltpu
from jax.sharding import PartitionSpec as P

BLOCK = 128
Y_LEVELS = 8
W_LEVELS = 7
EPSILON = 1e-06
LANES = 128
LARGE_COST = pl.CostEstimate(flops=2 * 10**11, bytes_accessed=1, transcendentals=0)
SMALL_COST = pl.CostEstimate(flops=1, bytes_accessed=1, transcendentals=0)
ANYWHERE = pl.BlockSpec(memory_space=pl.ANY)

CHUNKS = ((3, 3), (5, 5), (6, 6), (6, 6), (5, 5), (3, 3))
DIRECT_FROM = 3


def chunks_of(unit_count):
    units = unit_count // LANES
    if units == sum(a + b for a, b in CHUNKS):
        return CHUNKS
    count = (units - 2) // 4
    last = (units - 2 - 4 * count) // 2
    return ((1, 1),) + ((2, 2),) * count + (((last, last),) if last else ())


def params():
    return pltpu.CompilerParams(vmem_limit_bytes=64 * 1024 * 1024)


def code_rows(order, grad_out, grad_dither, own_rows, after=()):
    row_count = grad_out.shape[0]
    steps = order.shape[0]
    spec = pl.BlockSpec((row_count, own_rows), lambda i, order: (0, order[i]))

    def body(order_ref, grad_ref, dither_ref, *rest):
        for start in range(0, own_rows, BLOCK):
            grad = grad_ref[:, start : start + BLOCK].astype(jnp.float32)
            top = jnp.max(jnp.abs(grad), axis=1, keepdims=True)
            scale = ((top + EPSILON) / Y_LEVELS).astype(jnp.bfloat16).astype(jnp.float32)
            value = grad + dither_ref[:, start : start + BLOCK] * scale
            rest[-1][0, start : start + BLOCK, :] = value.astype(jnp.bfloat16).T

    return pl.pallas_call(
        body,
        grid_spec=pltpu.PrefetchScalarGridSpec(
            num_scalar_prefetch=1,
            grid=(steps,),
            in_specs=[spec, spec] + [ANYWHERE] * len(after),
            out_specs=pl.BlockSpec((1, own_rows, row_count), lambda i, order: (i, 0, 0)),
        ),
        out_shape=jax.ShapeDtypeStruct((steps, own_rows, row_count), jnp.bfloat16),
        compiler_params=params(),
        cost_estimate=SMALL_COST,
    )(order, grad_out, grad_dither, *after)


def column_block(rows, start, width):
    return pl.BlockSpec((pl.Element(rows), pl.Element(width)), lambda i, *_: (i * rows, start))


def cut_columns(values, spans, after=()):
    rows = values.shape[0]
    steps = 4

    def body(*refs):
        for in_ref, out_ref in zip(refs, refs[-len(spans) :]):
            out_ref[...] = in_ref[...]

    return pl.pallas_call(
        body,
        grid=(steps,),
        in_specs=[column_block(rows // steps, *span) for span in spans] + [ANYWHERE] * len(after),
        out_specs=[pl.BlockSpec((rows // steps, width), lambda i: (i, 0)) for _, width in spans],
        out_shape=[jax.ShapeDtypeStruct((rows, width), values.dtype) for _, width in spans],
        compiler_params=params(),
        cost_estimate=SMALL_COST,
    )(*[values] * len(spans), *after)


def joined(core, pieces):
    if len(pieces) == 1:
        return pieces[0][0]
    mine, other = (p[0] for p in pieces)
    return jnp.where(
        core == 0, jnp.concatenate([mine, other], axis=1), jnp.concatenate([other, mine], axis=1)
    )


def group_terms(y_block, acts, hidden, feature):
    rows, width = y_block.shape[0], acts.shape[1]
    partial = jnp.dot(y_block, acts, preferred_element_type=jnp.float32)
    column = jnp.broadcast_to(feature, (LANES, rows)).T
    wide = jnp.concatenate([column] * (width // LANES), axis=1)
    out = []
    for start in range(0, rows, BLOCK):
        piece = partial[start : start + BLOCK]
        top = jnp.max(jnp.abs(piece), axis=0, keepdims=True)
        scale = ((top + EPSILON) / W_LEVELS).astype(jnp.bfloat16).astype(jnp.float32)
        out.append(piece + (wide[start : start + BLOCK] + hidden) * scale)
    return jnp.concatenate(out, axis=0)


def pair_terms(owner, place, core, y0, y1, acts, acts0, acts1, dithers, start, ahead, after):
    steps, own_rows = y0[0].shape[:2]
    tokens, units = acts.shape
    half = steps // 2
    count, both = len(y0), len(y0) + len(y1)
    width = acts0.shape[1]

    def body(table_ref, *refs):
        refs = list(refs)
        y0_refs, y1_refs = refs[:count], refs[count : both]
        a0_ref, a1_ref, h0_ref, h1_ref, f0_ref, f1_ref = refs[both : both + 6]
        cut_refs = refs[both + 6 : both + 6 + len(ahead)]
        outs = refs[both + 6 + len(ahead) + len(after) :]
        core = table_ref[steps + half]
        for cut_ref, out_ref in zip(cut_refs, outs[2:]):
            out_ref[...] = cut_ref[...]
        columns = slice(start, start + width)
        mine = group_terms(joined(core, y0_refs), a0_ref[...], h0_ref[:, columns], f0_ref[...])
        other = group_terms(joined(core, y1_refs), a1_ref[...], h1_ref[:, columns], f1_ref[...])
        total = (mine + other).astype(jnp.bfloat16)
        step = pl.program_id(0)

        @pl.when(step < half)
        def _():
            outs[0][...] = total

        @pl.when(step >= half)
        def _():
            outs[1][...] = total


    y0_specs, y1_specs = (
        [pl.BlockSpec((1, own_rows, y.shape[2]), lambda i, t: (i, 0, 0)) for y in ys] for ys in (y0, y1)
    )
    f_spec = pl.BlockSpec((1, own_rows), lambda i, t: (0, units // own_rows + t[i]))
    h_spec = pl.BlockSpec((1, dithers[0].shape[1]), lambda i, t: (0, 0))
    a_spec = pl.BlockSpec((tokens, width), lambda i, t: (0, 0))
    out_specs = [
        pl.BlockSpec((own_rows, width), lambda i, t: (t[steps + jnp.minimum(i, half - 1)], 0)),
        pl.BlockSpec((own_rows, width), lambda i, t: (t[steps + jnp.maximum(i - half, 0)], 0)),
    ]
    out_shape = [jax.ShapeDtypeStruct((half * own_rows, width), jnp.bfloat16)] * 2
    for _, cut_width in ahead:
        out_specs.append(pl.BlockSpec((tokens // steps, cut_width), lambda i, t: (i, 0)))
        out_shape.append(jax.ShapeDtypeStruct((tokens, cut_width), acts.dtype))
    return pl.pallas_call(
        body,
        grid_spec=pltpu.PrefetchScalarGridSpec(
            num_scalar_prefetch=1,
            grid=(steps,),
            in_specs=[*y0_specs, *y1_specs, a_spec, a_spec, h_spec, h_spec, f_spec, f_spec]
            + [column_block(tokens // steps, *span) for span in ahead]
            + [ANYWHERE] * len(after),
            out_specs=out_specs,
        ),
        out_shape=out_shape,
        compiler_params=params(),
        cost_estimate=LARGE_COST,
    )(
        jnp.concatenate([owner, place, core[None]]),
        *y0, *y1, acts0, acts1, *dithers, *dithers, *[acts] * len(ahead), *after,
    )


def add_up(keeps, comes, pieces, after):
    rows = keeps[0].shape[0]
    widths = [k.shape[1] for k in keeps]
    steps = rows // LANES
    each = steps // pieces

    def body(*refs):
        outs = refs[-pieces:]
        for piece, out_ref in enumerate(outs):

            @pl.when(pl.program_id(0) // each == piece)
            def _(out_ref=out_ref):
                edge = 0
                for at, width in enumerate(widths):
                    keep, come = refs[2 * at], refs[2 * at + 1]
                    total = keep[...].astype(jnp.float32) + come[...].astype(jnp.float32)
                    out_ref[:, edge : edge + width] = total.astype(out_ref.dtype)
                    edge += width

    operands = [v for pair in zip(keeps, comes) for v in pair]
    return pl.pallas_call(
        body,
        grid=(steps,),
        in_specs=[pl.BlockSpec((LANES, v.shape[1]), lambda i: (i, 0)) for v in operands]
        + [ANYWHERE] * len(after),
        out_specs=[
            pl.BlockSpec(
                (LANES, sum(widths)), lambda i, p=p: (jnp.clip(i - p * each, 0, each - 1), 0)
            )
            for p in range(pieces)
        ],
        out_shape=[
            jax.ShapeDtypeStruct(
                (rows // pieces, sum(widths)), jnp.bfloat16 if p or pieces == 1 else jnp.float32
            )
            for p in range(pieces)
        ],
        compiler_params=params(),
        cost_estimate=SMALL_COST,
    )(*operands, *after)


def finish(start, parts, result, out_shape):
    own_rows, width = parts[0].shape
    given = [] if result is None else [result]

    def body(*refs):
        out_ref, held, sem = refs[-3:]
        total = refs[0][...].astype(jnp.float32)
        for ref in refs[1 : len(parts)]:
            total = total + ref[...].astype(jnp.float32)
        held[...] = total
        copy = pltpu.make_async_copy(held, out_ref.at[:, pl.ds(start, width)], sem)
        copy.start()
        copy.wait()

    return pl.pallas_call(
        body,
        in_specs=[pl.BlockSpec(memory_space=pltpu.VMEM)] * len(parts) + [ANYWHERE] * len(given),
        out_specs=ANYWHERE,
        out_shape=out_shape,
        scratch_shapes=[pltpu.VMEM((own_rows, width), jnp.float32), pltpu.SemaphoreType.DMA],
        input_output_aliases={len(parts): 0} if given else {},
        compiler_params=params(),
        cost_estimate=SMALL_COST,
    )(*parts, *given)


def per_device(grad_out, activations, grad_dither, hidden_dither, feature_dither):
    owners = lax.axis_size("dp")
    own_rows = grad_out.shape[1] // owners
    unit_count = activations.shape[1]
    me = lax.axis_index("dp").astype(jnp.int32)
    cores = lax.axis_size("tensor")
    core = lax.axis_index("tensor").astype(jnp.int32)
    pair_bits = (1, 2)
    lines = [[i for i in range(owners) if i % 4 == r] for r in range(4)]

    def exchange(value, bit):
        return lax.ppermute(value, "dp", [(i, i ^ bit) for i in range(owners)])

    def over_tokens(values):
        if cores == 2:
            return [values, lax.ppermute(values, "tensor", [(0, 1), (1, 0)])]
        return [lax.all_gather(values, "tensor", axis=2, tiled=True)]

    steps = chunks_of(unit_count)
    spans, at = [], 0
    for chunk in steps:
        spans.append([])
        for c in chunk:
            spans[-1].append((at, c * LANES))
            at += c * LANES

    count = owners // 4
    relative = jnp.arange(count, dtype=jnp.int32)
    absolute = relative ^ (me // 4)
    owner = []
    for part in range(2):
        mine = 4 * absolute + me % 4
        owner.append(jnp.concatenate([mine ^ pair_bits[1 - part], mine]))

    dithers = jnp.concatenate([hidden_dither, feature_dither], axis=1)
    dithers_other = [exchange(dithers, bit) for bit in pair_bits]
    first = cut_columns(activations, [*spans[0], *spans[1]], [dithers])
    cuts = {(at // 2, at % 2): values for at, values in enumerate(first)}
    acts_other = {key: exchange(values, pair_bits[key[1]]) for key, values in cuts.items()}
    y_other, y0, after = [], [], [first[0], *dithers_other]
    for part, bit in enumerate(pair_bits):
        y_send = code_rows(owner[part] ^ bit, grad_out, grad_dither, own_rows, after)
        y_other.append(exchange(y_send, bit))
        after = [y_send]
    for part in range(2):
        y_mine = code_rows(owner[part], grad_out, grad_dither, own_rows, after)
        y0.append(over_tokens(y_mine))
        after = [y_mine]
    after = [y_mine, y_other[1], acts_other[0, 1]]
    y1 = [over_tokens(y) for y in y_other]

    def sums_of(step, keeps, comes, after):
        if step < DIRECT_FROM:
            (terms,) = add_up(keeps, comes, 1, after)
            return [lax.psum_scatter(
                terms, "dp", scatter_dimension=0, axis_index_groups=lines, tiled=True
            )], terms
        mine, *others = add_up(keeps, comes, count, after)
        return [mine] + [exchange(v, 4 * (at + 1)) for at, v in enumerate(others)], mine

    result, waiting, before = None, [], []
    out_shape = jax.ShapeDtypeStruct((own_rows, unit_count), jnp.float32)
    keeps, comes = None, None
    for step in range(len(spans) + 1):
        keeps_now, comes_now = [], []
        for part in range(2):
            if part and step:
                if step - 1 > DIRECT_FROM:
                    result = finish(*waiting.pop(), result, out_shape)
                    after = after + [result]
                parts, made = sums_of(step - 1, keeps, comes, after)
                waiting.append((spans[step - 1][0][0], parts))
                after = [made]
            if step < len(spans):
                start, width = spans[step][part]
                ahead = spans[step + 2] if part and step + 2 < len(spans) else []
                send, keep, *cut = pair_terms(
                    owner[part], absolute if step < DIRECT_FROM else relative, core, y0[part],
                    y1[part], activations, cuts.pop((step, part)), acts_other.pop((step, part)),
                    [dithers, dithers_other[part]], start, ahead, after,
                )
                for p, columns in enumerate(cut):
                    cuts[step + 2, p] = columns
                    acts_other[step + 2, p] = exchange(columns, pair_bits[p])
                keeps_now.append(keep)
                comes_now.append(exchange(send, pair_bits[1 - part]))
                after = [send]
        keeps, comes = keeps_now, comes_now
    for start, parts in waiting:
        result = finish(start, parts, result, out_shape)
    return result


def solution(mesh):
    placed = (
        P(("dp", "tensor"), None),
        P("dp", "tensor"),
        P(("dp", "tensor"), None),
        P("dp", "tensor"),
        P("dp", None),
    )
    return jax.shard_map(
        per_device, mesh=mesh, in_specs=placed, out_specs=P("dp", "tensor"), check_vma=False
    )
```

```python
import jax
import jax.numpy as jnp
from jax import lax
from jax.experimental import pallas as pl
from jax.experimental.pallas import tpu as pltpu
from jax.sharding import PartitionSpec as P

BLOCK = 128
Y_LEVELS = 8
W_LEVELS = 7
EPSILON = 1e-06
LANES = 128
LARGE_COST = pl.CostEstimate(flops=2 * 10**11, bytes_accessed=1, transcendentals=0)
SMALL_COST = pl.CostEstimate(flops=1, bytes_accessed=1, transcendentals=0)
ANYWHERE = pl.BlockSpec(memory_space=pl.ANY)

CHUNKS = (4, 6, 10, 10, 10, 10, 6)


def chunks_of(unit_count):
    units = unit_count // LANES
    if units == sum(CHUNKS):
        return CHUNKS
    return (2,) + (4,) * ((units - 2) // 4) + (1,) * ((units - 2) % 4)


def params():
    return pltpu.CompilerParams(vmem_limit_bytes=64 * 1024 * 1024)


def code_rows(order, grad_out, grad_dither, own_rows, after=()):
    row_count = grad_out.shape[0]
    steps = order.shape[0]
    spec = pl.BlockSpec((row_count, own_rows), lambda i, order: (0, order[i]))

    def body(order_ref, grad_ref, dither_ref, *rest):
        for start in range(0, own_rows, BLOCK):
            grad = grad_ref[:, start : start + BLOCK].astype(jnp.float32)
            top = jnp.max(jnp.abs(grad), axis=1, keepdims=True)
            scale = ((top + EPSILON) / Y_LEVELS).astype(jnp.bfloat16).astype(jnp.float32)
            value = grad + dither_ref[:, start : start + BLOCK] * scale
            rest[-1][0, start : start + BLOCK, :] = value.astype(jnp.bfloat16).T

    return pl.pallas_call(
        body,
        grid_spec=pltpu.PrefetchScalarGridSpec(
            num_scalar_prefetch=1,
            grid=(steps,),
            in_specs=[spec, spec] + [ANYWHERE] * len(after),
            out_specs=pl.BlockSpec((1, own_rows, row_count), lambda i, order: (i, 0, 0)),
        ),
        out_shape=jax.ShapeDtypeStruct((steps, own_rows, row_count), jnp.bfloat16),
        compiler_params=params(),
        cost_estimate=SMALL_COST,
    )(order, grad_out, grad_dither, *after)


def column_block(rows, start, width):
    return pl.BlockSpec((pl.Element(rows), pl.Element(width)), lambda i, *_: (i * rows, start))


def cut_columns(values, spans, after=()):
    rows = values.shape[0]
    steps = 4

    def body(*refs):
        for in_ref, out_ref in zip(refs, refs[-len(spans) :]):
            out_ref[...] = in_ref[...]

    return pl.pallas_call(
        body,
        grid=(steps,),
        in_specs=[column_block(rows // steps, *span) for span in spans] + [ANYWHERE] * len(after),
        out_specs=[pl.BlockSpec((rows // steps, width), lambda i: (i, 0)) for _, width in spans],
        out_shape=[jax.ShapeDtypeStruct((rows, width), values.dtype) for _, width in spans],
        compiler_params=params(),
        cost_estimate=SMALL_COST,
    )(*[values] * len(spans), *after)


def joined(core, pieces):
    if len(pieces) == 1:
        return pieces[0][0]
    mine, other = (p[0] for p in pieces)
    return jnp.where(
        core == 0, jnp.concatenate([mine, other], axis=1), jnp.concatenate([other, mine], axis=1)
    )


def group_terms(y_block, acts, hidden, feature):
    rows, width = y_block.shape[0], acts.shape[1]
    partial = jnp.dot(y_block, acts, preferred_element_type=jnp.float32)
    column = jnp.broadcast_to(feature, (LANES, rows)).T
    wide = jnp.concatenate([column] * (width // LANES), axis=1)
    out = []
    for start in range(0, rows, BLOCK):
        piece = partial[start : start + BLOCK]
        top = jnp.max(jnp.abs(piece), axis=0, keepdims=True)
        scale = ((top + EPSILON) / W_LEVELS).astype(jnp.bfloat16).astype(jnp.float32)
        out.append(piece + (wide[start : start + BLOCK] + hidden) * scale)
    return jnp.concatenate(out, axis=0)


def pair_terms(owner, place, core, y0, y1, acts, acts0, acts1, dithers, start, ahead, after):
    steps, own_rows = y0[0].shape[:2]
    tokens, units = acts.shape
    half = steps // 2
    count, both = len(y0), len(y0) + len(y1)
    width = acts0.shape[1]

    def body(table_ref, *refs):
        refs = list(refs)
        y0_refs, y1_refs = refs[:count], refs[count : both]
        a0_ref, a1_ref, h0_ref, h1_ref, f0_ref, f1_ref = refs[both : both + 6]
        cut_refs = refs[both + 6 : both + 6 + len(ahead)]
        outs = refs[both + 6 + len(ahead) + len(after) :]
        core = table_ref[steps + half]
        for cut_ref, out_ref in zip(cut_refs, outs[2:]):
            out_ref[...] = cut_ref[...]
        columns = slice(start, start + width)
        mine = group_terms(joined(core, y0_refs), a0_ref[...], h0_ref[:, columns], f0_ref[...])
        other = group_terms(joined(core, y1_refs), a1_ref[...], h1_ref[:, columns], f1_ref[...])
        total = (mine + other).astype(jnp.bfloat16)
        step = pl.program_id(0)

        @pl.when(step < half)
        def _():
            outs[0][...] = total

        @pl.when(step >= half)
        def _():
            outs[1][...] = total


    y0_specs, y1_specs = (
        [pl.BlockSpec((1, own_rows, y.shape[2]), lambda i, t: (i, 0, 0)) for y in ys] for ys in (y0, y1)
    )
    f_spec = pl.BlockSpec((1, own_rows), lambda i, t: (0, units // own_rows + t[i]))
    h_spec = pl.BlockSpec((1, dithers[0].shape[1]), lambda i, t: (0, 0))
    a_spec = pl.BlockSpec((tokens, width), lambda i, t: (0, 0))
    out_specs = [
        pl.BlockSpec((own_rows, width), lambda i, t: (t[steps + jnp.minimum(i, half - 1)], 0)),
        pl.BlockSpec((own_rows, width), lambda i, t: (t[steps + jnp.maximum(i - half, 0)], 0)),
    ]
    out_shape = [jax.ShapeDtypeStruct((half * own_rows, width), jnp.bfloat16)] * 2
    for _, cut_width in ahead:
        out_specs.append(pl.BlockSpec((tokens // steps, cut_width), lambda i, t: (i, 0)))
        out_shape.append(jax.ShapeDtypeStruct((tokens, cut_width), acts.dtype))
    return pl.pallas_call(
        body,
        grid_spec=pltpu.PrefetchScalarGridSpec(
            num_scalar_prefetch=1,
            grid=(steps,),
            in_specs=[*y0_specs, *y1_specs, a_spec, a_spec, h_spec, h_spec, f_spec, f_spec]
            + [column_block(tokens // steps, *span) for span in ahead]
            + [ANYWHERE] * len(after),
            out_specs=out_specs,
        ),
        out_shape=out_shape,
        compiler_params=params(),
        cost_estimate=LARGE_COST,
    )(
        jnp.concatenate([owner, place, core[None]]),
        *y0, *y1, acts0, acts1, *dithers, *dithers, *[acts] * len(ahead), *after,
    )


def add_up(keep, come, after):
    rows, width = keep.shape

    def body(keep_ref, come_ref, *rest):
        total = keep_ref[...].astype(jnp.float32) + come_ref[...].astype(jnp.float32)
        rest[-1][...] = total.astype(jnp.bfloat16)

    spec = pl.BlockSpec((2 * LANES, width), lambda i: (i, 0))
    return pl.pallas_call(
        body,
        grid=(rows // (2 * LANES),),
        in_specs=[spec, spec] + [ANYWHERE] * len(after),
        out_specs=spec,
        out_shape=jax.ShapeDtypeStruct((rows, width), jnp.bfloat16),
        compiler_params=params(),
        cost_estimate=SMALL_COST,
    )(keep, come, *after)


def finish(start, parts, result, out_shape):
    own_rows, width = parts[0].shape
    given = [] if result is None else [result]

    def body(*refs):
        out_ref, held, sem = refs[-3:]
        total = refs[0][...].astype(jnp.float32)
        for ref in refs[1 : len(parts)]:
            total = total + ref[...].astype(jnp.float32)
        held[...] = total
        copy = pltpu.make_async_copy(held, out_ref.at[:, pl.ds(start, width)], sem)
        copy.start()
        copy.wait()

    return pl.pallas_call(
        body,
        in_specs=[pl.BlockSpec(memory_space=pltpu.VMEM)] * len(parts) + [ANYWHERE] * len(given),
        out_specs=ANYWHERE,
        out_shape=out_shape,
        scratch_shapes=[pltpu.VMEM((own_rows, width), jnp.float32), pltpu.SemaphoreType.DMA],
        input_output_aliases={len(parts): 0} if given else {},
        compiler_params=params(),
        cost_estimate=SMALL_COST,
    )(*parts, *given)


def per_device(grad_out, activations, grad_dither, hidden_dither, feature_dither):
    owners = lax.axis_size("dp")
    own_rows = grad_out.shape[1] // owners
    unit_count = activations.shape[1]
    me = lax.axis_index("dp").astype(jnp.int32)
    cores = lax.axis_size("tensor")
    core = lax.axis_index("tensor").astype(jnp.int32)
    pair_bit, half_bit = 1, 2
    lines = [[i for i in range(owners) if i % 4 == r] for r in range(4)]

    def exchange(value, bit):
        return lax.ppermute(value, "dp", [(i, i ^ bit) for i in range(owners)])

    def over_tokens(values):
        if cores == 2:
            return [values, lax.ppermute(values, "tensor", [(0, 1), (1, 0)])]
        return [lax.all_gather(values, "tensor", axis=2, tiled=True)]

    spans, at = [], 0
    for c in chunks_of(unit_count):
        spans.append((at, c * LANES))
        at += c * LANES

    place = jnp.arange(owners // 4, dtype=jnp.int32)
    mine = 4 * place + me % 4
    owner = jnp.concatenate([mine ^ half_bit, mine])

    dithers = jnp.concatenate([hidden_dither, feature_dither], axis=1)
    dithers_other = exchange(dithers, pair_bit)
    cuts = dict(enumerate(cut_columns(activations, spans[:2], [dithers])))
    acts_other = {key: exchange(values, pair_bit) for key, values in cuts.items()}
    y_send = code_rows(owner ^ pair_bit, grad_out, grad_dither, own_rows, [cuts[0], dithers_other])
    y_other = exchange(y_send, pair_bit)
    y_mine = code_rows(owner, grad_out, grad_dither, own_rows, [y_send])
    y0 = over_tokens(y_mine)
    y1 = over_tokens(y_other)

    result, waiting = None, []
    out_shape = jax.ShapeDtypeStruct((own_rows, unit_count), jnp.float32)
    after, keep, come = [y_mine], None, None
    for chunk in range(len(spans) + 1):
        keep_now = come_now = None
        if chunk < len(spans):
            start, width = spans[chunk]
            ahead = spans[chunk + 2 : chunk + 3]
            send, keep_now, *cut = pair_terms(
                owner, place, core, y0, y1, activations, cuts.pop(chunk), acts_other.pop(chunk),
                [dithers, dithers_other], start, ahead, after,
            )
            come_now = exchange(send, half_bit)
            for columns in cut:
                cuts[chunk + 2] = columns
                acts_other[chunk + 2] = exchange(columns, pair_bit)
            after = [send]
        if chunk:
            terms = add_up(keep, come, after)
            after = [terms]
            waiting.append((spans[chunk - 1][0], [lax.psum_scatter(
                terms, "dp", scatter_dimension=0, axis_index_groups=lines, tiled=True
            )]))
        keep, come = keep_now, come_now
    for start, parts in waiting:
        result = finish(start, parts, result, out_shape)
    return result


def solution(mesh):
    placed = (
        P(("dp", "tensor"), None),
        P("dp", "tensor"),
        P(("dp", "tensor"), None),
        P("dp", "tensor"),
        P("dp", None),
    )
    return jax.shard_map(
        per_device, mesh=mesh, in_specs=placed, out_specs=P("dp", "tensor"), check_vma=False
    )
```

```python
import jax
import jax.numpy as jnp
from jax import lax
from jax.experimental import pallas as pl
from jax.experimental.pallas import tpu as pltpu
from jax.sharding import PartitionSpec as P

BLOCK = 128
Y_LEVELS = 8
W_LEVELS = 7
EPSILON = 1e-06
LANES = 128
LARGE_COST = pl.CostEstimate(flops=2 * 10**11, bytes_accessed=1, transcendentals=0)
SMALL_COST = pl.CostEstimate(flops=1, bytes_accessed=1, transcendentals=0)
ANYWHERE = pl.BlockSpec(memory_space=pl.ANY)

CHUNKS = (4, 6, 10, 10, 10)
LAST = 16


def chunks_of(unit_count):
    units = unit_count // LANES
    if units == sum(CHUNKS) + LAST:
        return CHUNKS, LAST
    last = max(units // 4, 1)
    rest = units - last
    return (rest - 4 * (rest // 5),) + (rest // 5,) * 4, last


def params():
    return pltpu.CompilerParams(vmem_limit_bytes=64 * 1024 * 1024)


def code_rows(order, grad_out, grad_dither, own_rows, after=()):
    row_count = grad_out.shape[0]
    steps = order.shape[0]
    spec = pl.BlockSpec((row_count, own_rows), lambda i, order: (0, order[i]))

    def body(order_ref, grad_ref, dither_ref, *rest):
        for start in range(0, own_rows, BLOCK):
            grad = grad_ref[:, start : start + BLOCK].astype(jnp.float32)
            top = jnp.max(jnp.abs(grad), axis=1, keepdims=True)
            scale = ((top + EPSILON) / Y_LEVELS).astype(jnp.bfloat16).astype(jnp.float32)
            value = grad + dither_ref[:, start : start + BLOCK] * scale
            rest[-1][0, start : start + BLOCK, :] = value.astype(jnp.bfloat16).T

    return pl.pallas_call(
        body,
        grid_spec=pltpu.PrefetchScalarGridSpec(
            num_scalar_prefetch=1,
            grid=(steps,),
            in_specs=[spec, spec] + [ANYWHERE] * len(after),
            out_specs=pl.BlockSpec((1, own_rows, row_count), lambda i, order: (i, 0, 0)),
        ),
        out_shape=jax.ShapeDtypeStruct((steps, own_rows, row_count), jnp.bfloat16),
        compiler_params=params(),
        cost_estimate=SMALL_COST,
    )(order, grad_out, grad_dither, *after)


def column_block(rows, start, width):
    return pl.BlockSpec((pl.Element(rows), pl.Element(width)), lambda i, *_: (i * rows, start))


def cut_columns(values, spans, after=()):
    rows = values.shape[0]
    steps = 4

    def body(*refs):
        for in_ref, out_ref in zip(refs, refs[-len(spans) :]):
            out_ref[...] = in_ref[...]

    return pl.pallas_call(
        body,
        grid=(steps,),
        in_specs=[column_block(rows // steps, *span) for span in spans] + [ANYWHERE] * len(after),
        out_specs=[pl.BlockSpec((rows // steps, width), lambda i: (i, 0)) for _, width in spans],
        out_shape=[jax.ShapeDtypeStruct((rows, width), values.dtype) for _, width in spans],
        compiler_params=params(),
        cost_estimate=SMALL_COST,
    )(*[values] * len(spans), *after)


def joined(core, pieces):
    if len(pieces) == 1:
        return pieces[0][0]
    mine, other = (p[0] for p in pieces)
    return jnp.where(
        core == 0, jnp.concatenate([mine, other], axis=1), jnp.concatenate([other, mine], axis=1)
    )


def group_terms(y_block, acts, hidden, feature):
    rows, width = y_block.shape[0], acts.shape[1]
    partial = jnp.dot(y_block, acts, preferred_element_type=jnp.float32)
    column = jnp.broadcast_to(feature, (LANES, rows)).T
    wide = jnp.concatenate([column] * (width // LANES), axis=1)
    out = []
    for start in range(0, rows, BLOCK):
        piece = partial[start : start + BLOCK]
        top = jnp.max(jnp.abs(piece), axis=0, keepdims=True)
        scale = ((top + EPSILON) / W_LEVELS).astype(jnp.bfloat16).astype(jnp.float32)
        out.append(piece + (wide[start : start + BLOCK] + hidden) * scale)
    return jnp.concatenate(out, axis=0)


def pair_terms(owner, place, core, y0, y1, acts, acts0, acts1, dithers, start, ahead, after):
    steps, own_rows = y0[0].shape[:2]
    tokens, units = acts.shape
    half = steps // 2
    count, both = len(y0), len(y0) + len(y1)
    width = acts0.shape[1]

    def body(table_ref, *refs):
        refs = list(refs)
        y0_refs, y1_refs = refs[:count], refs[count : both]
        a0_ref, a1_ref, h0_ref, h1_ref, f0_ref, f1_ref = refs[both : both + 6]
        cut_refs = refs[both + 6 : both + 6 + len(ahead)]
        outs = refs[both + 6 + len(ahead) + len(after) :]
        core = table_ref[steps + half]
        for cut_ref, out_ref in zip(cut_refs, outs[2:]):
            out_ref[...] = cut_ref[...]
        columns = slice(start, start + width)
        mine = group_terms(joined(core, y0_refs), a0_ref[...], h0_ref[:, columns], f0_ref[...])
        other = group_terms(joined(core, y1_refs), a1_ref[...], h1_ref[:, columns], f1_ref[...])
        total = (mine + other).astype(jnp.bfloat16)
        step = pl.program_id(0)

        @pl.when(step < half)
        def _():
            outs[0][...] = total

        @pl.when(step >= half)
        def _():
            outs[1][...] = total


    y0_specs, y1_specs = (
        [pl.BlockSpec((1, own_rows, y.shape[2]), lambda i, t: (i, 0, 0)) for y in ys] for ys in (y0, y1)
    )
    f_spec = pl.BlockSpec((1, own_rows), lambda i, t: (0, units // own_rows + t[i]))
    h_spec = pl.BlockSpec((1, dithers[0].shape[1]), lambda i, t: (0, 0))
    a_spec = pl.BlockSpec((tokens, width), lambda i, t: (0, 0))
    out_specs = [
        pl.BlockSpec((own_rows, width), lambda i, t: (t[steps + jnp.minimum(i, half - 1)], 0)),
        pl.BlockSpec((own_rows, width), lambda i, t: (t[steps + jnp.maximum(i - half, 0)], 0)),
    ]
    out_shape = [jax.ShapeDtypeStruct((half * own_rows, width), jnp.bfloat16)] * 2
    for _, cut_width in ahead:
        out_specs.append(pl.BlockSpec((tokens // steps, cut_width), lambda i, t: (i, 0)))
        out_shape.append(jax.ShapeDtypeStruct((tokens, cut_width), acts.dtype))
    return pl.pallas_call(
        body,
        grid_spec=pltpu.PrefetchScalarGridSpec(
            num_scalar_prefetch=1,
            grid=(steps,),
            in_specs=[*y0_specs, *y1_specs, a_spec, a_spec, h_spec, h_spec, f_spec, f_spec]
            + [column_block(tokens // steps, *span) for span in ahead]
            + [ANYWHERE] * len(after),
            out_specs=out_specs,
        ),
        out_shape=out_shape,
        compiler_params=params(),
        cost_estimate=LARGE_COST,
    )(
        jnp.concatenate([owner, place, core[None]]),
        *y0, *y1, acts0, acts1, *dithers, *dithers, *[acts] * len(ahead), *after,
    )


def add_up(keep, come, after, cost):
    rows, width = keep.shape

    def body(keep_ref, come_ref, *rest):
        total = keep_ref[...].astype(jnp.float32) + come_ref[...].astype(jnp.float32)
        rest[-1][...] = total.astype(jnp.bfloat16)

    spec = pl.BlockSpec((2 * LANES, width), lambda i: (i, 0))
    return pl.pallas_call(
        body,
        grid=(rows // (2 * LANES),),
        in_specs=[spec, spec] + [ANYWHERE] * len(after),
        out_specs=spec,
        out_shape=jax.ShapeDtypeStruct((rows, width), jnp.bfloat16),
        compiler_params=params(),
        cost_estimate=cost,
    )(keep, come, *after)


def halve(keep, come, after):
    rows, width = keep.shape
    half = rows // (2 * LANES)

    def body(keep_ref, come_ref, *rest):
        total = keep_ref[...].astype(jnp.float32) + come_ref[...].astype(jnp.float32)
        step = pl.program_id(0)

        @pl.when(step < half)
        def _():
            rest[-2][...] = total.astype(jnp.bfloat16)

        @pl.when(step >= half)
        def _():
            rest[-1][...] = total.astype(jnp.bfloat16)

    spec = pl.BlockSpec((LANES, width), lambda i: (jnp.where(i < half, i + half, i - half), 0))
    return pl.pallas_call(
        body,
        grid=(2 * half,),
        in_specs=[spec, spec] + [ANYWHERE] * len(after),
        out_specs=[
            pl.BlockSpec((LANES, width), lambda i: (jnp.minimum(i, half - 1), 0)),
            pl.BlockSpec((LANES, width), lambda i: (jnp.maximum(i - half, 0), 0)),
        ],
        out_shape=[jax.ShapeDtypeStruct((rows // 2, width), jnp.bfloat16)] * 2,
        compiler_params=params(),
        cost_estimate=SMALL_COST,
    )(keep, come, *after)


def hold(value, after):
    def body(*refs):
        del refs

    return pl.pallas_call(
        body,
        in_specs=[ANYWHERE] * (1 + len(after)),
        out_specs=ANYWHERE,
        out_shape=jax.ShapeDtypeStruct(value.shape, value.dtype),
        input_output_aliases={0: 0},
        compiler_params=params(),
        cost_estimate=SMALL_COST,
    )(value, *after)


def relative_order(bits):
    order = [0]
    for bit in reversed(bits):
        order = order + [bit | r for r in order]
    return order


def finish(start, parts, result, out_shape):
    own_rows, width = parts[0].shape
    given = [] if result is None else [result]

    def body(*refs):
        out_ref, held, sem = refs[-3:]
        total = refs[0][...].astype(jnp.float32)
        for ref in refs[1 : len(parts)]:
            total = total + ref[...].astype(jnp.float32)
        held[...] = total
        copy = pltpu.make_async_copy(held, out_ref.at[:, pl.ds(start, width)], sem)
        copy.start()
        copy.wait()

    return pl.pallas_call(
        body,
        in_specs=[pl.BlockSpec(memory_space=pltpu.VMEM)] * len(parts) + [ANYWHERE] * len(given),
        out_specs=ANYWHERE,
        out_shape=out_shape,
        scratch_shapes=[pltpu.VMEM((own_rows, width), jnp.float32), pltpu.SemaphoreType.DMA],
        input_output_aliases={len(parts): 0} if given else {},
        compiler_params=params(),
        cost_estimate=SMALL_COST,
    )(*parts, *given)


def per_device(grad_out, activations, grad_dither, hidden_dither, feature_dither):
    owners = lax.axis_size("dp")
    own_rows = grad_out.shape[1] // owners
    unit_count = activations.shape[1]
    me = lax.axis_index("dp").astype(jnp.int32)
    cores = lax.axis_size("tensor")
    core = lax.axis_index("tensor").astype(jnp.int32)
    pair_bit, half_bit = 1, 2
    lines = [[i for i in range(owners) if i % 4 == r] for r in range(4)]

    def exchange(value, bit):
        return lax.ppermute(value, "dp", [(i, i ^ bit) for i in range(owners)])

    def over_tokens(values):
        if cores == 2:
            return [values, lax.ppermute(values, "tensor", [(0, 1), (1, 0)])]
        return [lax.all_gather(values, "tensor", axis=2, tiled=True)]

    spans, at = [], 0
    chunks, last = chunks_of(unit_count)
    for c in (*chunks, last):
        spans.append((at, c * LANES))
        at += c * LANES
    last_span = spans.pop()

    place = jnp.arange(owners // 4, dtype=jnp.int32)
    mine = 4 * place + me % 4
    owner = jnp.concatenate([mine ^ half_bit, mine])

    last_bit = 4
    last_bits = [b for b in (1 << i for i in range(owners.bit_length() - 1)) if b != last_bit]
    order = relative_order(last_bits)
    order = order[len(order) // 2 :] + order[: len(order) // 2]
    last_owner = jnp.array(order, jnp.int32) ^ me
    last_place = jnp.arange(owners // 4, dtype=jnp.int32)

    dithers = jnp.concatenate([hidden_dither, feature_dither], axis=1)
    dithers_other = exchange(dithers, pair_bit)
    last_dithers = exchange(dithers, last_bit)
    *first, last_cut = cut_columns(activations, [*spans[:2], last_span], [dithers])
    cuts = dict(enumerate(first))
    last_acts = exchange(last_cut, last_bit)
    acts_other = {key: exchange(values, pair_bit) for key, values in cuts.items()}
    y_send = code_rows(
        owner ^ pair_bit, grad_out, grad_dither, own_rows, [cuts[0], dithers_other, last_dithers]
    )
    y_other = exchange(y_send, pair_bit)
    y_mine = code_rows(owner, grad_out, grad_dither, own_rows, [y_send])
    y0 = over_tokens(y_mine)
    last_y_send = code_rows(last_owner ^ last_bit, grad_out, grad_dither, own_rows, [y_mine])
    last_y_other = exchange(last_y_send, last_bit)
    last_y_mine = code_rows(last_owner, grad_out, grad_dither, own_rows, [last_y_send])
    y1 = over_tokens(y_other)

    result, waiting = None, []
    out_shape = jax.ShapeDtypeStruct((own_rows, unit_count), jnp.float32)
    after, keep, come = [last_y_mine, last_acts], None, None
    last_at = 3
    for chunk in range(len(spans) + 1):
        keep_now = come_now = None
        if chunk < len(spans):
            start, width = spans[chunk]
            ahead = spans[chunk + 2 : chunk + 3]
            if chunk == 2:
                after = after + [last_y_other]
            send, keep_now, *cut = pair_terms(
                owner, place, core, y0, y1, activations, cuts.pop(chunk), acts_other.pop(chunk),
                [dithers, dithers_other], start, ahead, after,
            )
            come_now = exchange(send, half_bit)
            for columns in cut:
                cuts[chunk + 2] = columns
                acts_other[chunk + 2] = exchange(columns, pair_bit)
            after = [send]
            if chunk == 1:
                last_y1 = over_tokens(hold(last_y_other, after))
            if chunk == last_at:
                last_send, last_keep = pair_terms(
                    last_owner, last_place, core, over_tokens(last_y_mine), last_y1,
                    activations, last_cut, last_acts, [dithers, last_dithers], last_span[0], [], after,
                )
                last_come = exchange(last_send, last_bits[0])
                after = [last_send]
        else:
            last_send, last_keep = halve(last_keep, last_come, after)
            last_come = exchange(last_send, last_bits[1])
            after = [last_send]
        if chunk:
            cost = LARGE_COST if chunk == len(spans) else SMALL_COST
            terms = add_up(keep, come, after, cost)
            after = [terms]
            waiting.append((spans[chunk - 1][0], [lax.psum_scatter(
                terms, "dp", scatter_dimension=0, axis_index_groups=lines, tiled=True
            )]))
        keep, come = keep_now, come_now
    for bit in last_bits[2:]:
        last_send, last_keep = halve(last_keep, last_come, after)
        last_come = exchange(last_send, bit)
        after = [last_send]
    waiting.append((last_span[0], [last_keep, last_come]))
    for start, parts in waiting:
        result = finish(start, parts, result, out_shape)
    return result


def solution(mesh):
    placed = (
        P(("dp", "tensor"), None),
        P("dp", "tensor"),
        P(("dp", "tensor"), None),
        P("dp", "tensor"),
        P("dp", None),
    )
    return jax.shard_map(
        per_device, mesh=mesh, in_specs=placed, out_specs=P("dp", "tensor"), check_vma=False
    )
```

```python
import jax
import jax.numpy as jnp
from jax import lax
from jax.experimental import pallas as pl
from jax.experimental.pallas import tpu as pltpu
from jax.sharding import PartitionSpec as P

BLOCK = 128
Y_LEVELS = 8
W_LEVELS = 7
EPSILON = 1e-06
LANES = 128
LARGE_COST = pl.CostEstimate(flops=2 * 10**11, bytes_accessed=1, transcendentals=0)
SMALL_COST = pl.CostEstimate(flops=1, bytes_accessed=1, transcendentals=0)
ANYWHERE = pl.BlockSpec(memory_space=pl.ANY)

CHUNKS = (4, 6, 10, 10, 10)
LAST = (8, 8)


def chunks_of(unit_count):
    units = unit_count // LANES
    if units == sum(CHUNKS) + sum(LAST):
        return CHUNKS, LAST
    last = max(units // 8, 1)
    rest = units - 2 * last
    return (rest - 4 * (rest // 5),) + (rest // 5,) * 4, (last, last)


def params():
    return pltpu.CompilerParams(vmem_limit_bytes=64 * 1024 * 1024)


def code_rows(order, grad_out, grad_dither, own_rows, after=()):
    row_count = grad_out.shape[0]
    steps = order.shape[0]
    spec = pl.BlockSpec((row_count, own_rows), lambda i, order: (0, order[i]))

    def body(order_ref, grad_ref, dither_ref, *rest):
        for start in range(0, own_rows, BLOCK):
            grad = grad_ref[:, start : start + BLOCK].astype(jnp.float32)
            top = jnp.max(jnp.abs(grad), axis=1, keepdims=True)
            scale = ((top + EPSILON) / Y_LEVELS).astype(jnp.bfloat16).astype(jnp.float32)
            value = grad + dither_ref[:, start : start + BLOCK] * scale
            rest[-1][0, start : start + BLOCK, :] = value.astype(jnp.bfloat16).T

    return pl.pallas_call(
        body,
        grid_spec=pltpu.PrefetchScalarGridSpec(
            num_scalar_prefetch=1,
            grid=(steps,),
            in_specs=[spec, spec] + [ANYWHERE] * len(after),
            out_specs=pl.BlockSpec((1, own_rows, row_count), lambda i, order: (i, 0, 0)),
        ),
        out_shape=jax.ShapeDtypeStruct((steps, own_rows, row_count), jnp.bfloat16),
        compiler_params=params(),
        cost_estimate=SMALL_COST,
    )(order, grad_out, grad_dither, *after)


def column_block(rows, start, width):
    return pl.BlockSpec((pl.Element(rows), pl.Element(width)), lambda i, *_: (i * rows, start))


def cut_columns(values, spans, after=()):
    rows = values.shape[0]
    steps = 4

    def body(*refs):
        for in_ref, out_ref in zip(refs, refs[-len(spans) :]):
            out_ref[...] = in_ref[...]

    return pl.pallas_call(
        body,
        grid=(steps,),
        in_specs=[column_block(rows // steps, *span) for span in spans] + [ANYWHERE] * len(after),
        out_specs=[pl.BlockSpec((rows // steps, width), lambda i: (i, 0)) for _, width in spans],
        out_shape=[jax.ShapeDtypeStruct((rows, width), values.dtype) for _, width in spans],
        compiler_params=params(),
        cost_estimate=SMALL_COST,
    )(*[values] * len(spans), *after)


def joined(core, pieces):
    if len(pieces) == 1:
        return pieces[0][0]
    mine, other = (p[0] for p in pieces)
    return jnp.where(
        core == 0, jnp.concatenate([mine, other], axis=1), jnp.concatenate([other, mine], axis=1)
    )


def group_terms(y_block, acts, hidden, feature):
    rows, width = y_block.shape[0], acts.shape[1]
    partial = jnp.dot(y_block, acts, preferred_element_type=jnp.float32)
    column = jnp.broadcast_to(feature, (LANES, rows)).T
    wide = jnp.concatenate([column] * (width // LANES), axis=1)
    out = []
    for start in range(0, rows, BLOCK):
        piece = partial[start : start + BLOCK]
        top = jnp.max(jnp.abs(piece), axis=0, keepdims=True)
        scale = ((top + EPSILON) / W_LEVELS).astype(jnp.bfloat16).astype(jnp.float32)
        out.append(piece + (wide[start : start + BLOCK] + hidden) * scale)
    return jnp.concatenate(out, axis=0)


def pair_terms(
    owner, place, core, y0, y1, acts, acts0, acts1, dithers, start, width, block, ahead, after
):
    steps, own_rows = y0[0].shape[:2]
    tokens, units = acts.shape
    half = steps // 2
    count, both = len(y0), len(y0) + len(y1)

    def body(table_ref, *refs):
        refs = list(refs)
        y0_refs, y1_refs = refs[:count], refs[count : both]
        a0_ref, a1_ref, h0_ref, h1_ref, f0_ref, f1_ref = refs[both : both + 6]
        cut_refs = refs[both + 6 : both + 6 + len(ahead)]
        outs = refs[both + 6 + len(ahead) + len(after) :]
        core = table_ref[steps + half]
        for cut_ref, out_ref in zip(cut_refs, outs[2:]):
            out_ref[...] = cut_ref[...]
        columns = slice(start, start + width)
        mine = group_terms(joined(core, y0_refs), a0_ref[...], h0_ref[:, columns], f0_ref[...])
        other = group_terms(joined(core, y1_refs), a1_ref[...], h1_ref[:, columns], f1_ref[...])
        total = (mine + other).astype(jnp.bfloat16)
        step = pl.program_id(0)

        @pl.when(step < half)
        def _():
            outs[0][...] = total

        @pl.when(step >= half)
        def _():
            outs[1][...] = total


    y0_specs, y1_specs = (
        [pl.BlockSpec((1, own_rows, y.shape[2]), lambda i, t: (i, 0, 0)) for y in ys] for ys in (y0, y1)
    )
    f_spec = pl.BlockSpec((1, own_rows), lambda i, t: (0, units // own_rows + t[i]))
    h_spec = pl.BlockSpec((1, dithers[0].shape[1]), lambda i, t: (0, 0))
    a_spec = pl.BlockSpec((tokens, width), lambda i, t: (0, block))
    out_specs = [
        pl.BlockSpec((own_rows, width), lambda i, t: (t[steps + jnp.minimum(i, half - 1)], 0)),
        pl.BlockSpec((own_rows, width), lambda i, t: (t[steps + jnp.maximum(i - half, 0)], 0)),
    ]
    out_shape = [jax.ShapeDtypeStruct((half * own_rows, width), jnp.bfloat16)] * 2
    for _, cut_width in ahead:
        out_specs.append(pl.BlockSpec((tokens // steps, cut_width), lambda i, t: (i, 0)))
        out_shape.append(jax.ShapeDtypeStruct((tokens, cut_width), acts.dtype))
    return pl.pallas_call(
        body,
        grid_spec=pltpu.PrefetchScalarGridSpec(
            num_scalar_prefetch=1,
            grid=(steps,),
            in_specs=[*y0_specs, *y1_specs, a_spec, a_spec, h_spec, h_spec, f_spec, f_spec]
            + [column_block(tokens // steps, *span) for span in ahead]
            + [ANYWHERE] * len(after),
            out_specs=out_specs,
        ),
        out_shape=out_shape,
        compiler_params=params(),
        cost_estimate=LARGE_COST,
    )(
        jnp.concatenate([owner, place, core[None]]),
        *y0, *y1, acts0, acts1, *dithers, *dithers, *[acts] * len(ahead), *after,
    )


def add_up(keep, come, after, cost):
    rows, width = keep.shape

    def body(keep_ref, come_ref, *rest):
        total = keep_ref[...].astype(jnp.float32) + come_ref[...].astype(jnp.float32)
        rest[-1][...] = total.astype(jnp.bfloat16)

    spec = pl.BlockSpec((2 * LANES, width), lambda i: (i, 0))
    return pl.pallas_call(
        body,
        grid=(rows // (2 * LANES),),
        in_specs=[spec, spec] + [ANYWHERE] * len(after),
        out_specs=spec,
        out_shape=jax.ShapeDtypeStruct((rows, width), jnp.bfloat16),
        compiler_params=params(),
        cost_estimate=cost,
    )(keep, come, *after)


def halve(keep, come, after, cost):
    rows, width = keep.shape
    half = rows // (2 * LANES)

    def body(keep_ref, come_ref, *rest):
        total = keep_ref[...].astype(jnp.float32) + come_ref[...].astype(jnp.float32)
        step = pl.program_id(0)

        @pl.when(step < half)
        def _():
            rest[-2][...] = total.astype(jnp.bfloat16)

        @pl.when(step >= half)
        def _():
            rest[-1][...] = total.astype(jnp.bfloat16)

    spec = pl.BlockSpec((LANES, width), lambda i: (jnp.where(i < half, i + half, i - half), 0))
    return pl.pallas_call(
        body,
        grid=(2 * half,),
        in_specs=[spec, spec] + [ANYWHERE] * len(after),
        out_specs=[
            pl.BlockSpec((LANES, width), lambda i: (jnp.minimum(i, half - 1), 0)),
            pl.BlockSpec((LANES, width), lambda i: (jnp.maximum(i - half, 0), 0)),
        ],
        out_shape=[jax.ShapeDtypeStruct((rows // 2, width), jnp.bfloat16)] * 2,
        compiler_params=params(),
        cost_estimate=cost,
    )(keep, come, *after)


def hold(value, after):
    def body(*refs):
        del refs

    return pl.pallas_call(
        body,
        in_specs=[ANYWHERE] * (1 + len(after)),
        out_specs=ANYWHERE,
        out_shape=jax.ShapeDtypeStruct(value.shape, value.dtype),
        input_output_aliases={0: 0},
        compiler_params=params(),
        cost_estimate=SMALL_COST,
    )(value, *after)


def relative_order(bits):
    order = [0]
    for bit in reversed(bits):
        order = order + [bit | r for r in order]
    return order


def finish(start, parts, result, out_shape):
    own_rows, width = parts[0].shape
    given = [] if result is None else [result]

    def body(*refs):
        out_ref, held, sem = refs[-3:]
        total = refs[0][...].astype(jnp.float32)
        for ref in refs[1 : len(parts)]:
            total = total + ref[...].astype(jnp.float32)
        held[...] = total
        copy = pltpu.make_async_copy(held, out_ref.at[:, pl.ds(start, width)], sem)
        copy.start()
        copy.wait()

    return pl.pallas_call(
        body,
        in_specs=[pl.BlockSpec(memory_space=pltpu.VMEM)] * len(parts) + [ANYWHERE] * len(given),
        out_specs=ANYWHERE,
        out_shape=out_shape,
        scratch_shapes=[pltpu.VMEM((own_rows, width), jnp.float32), pltpu.SemaphoreType.DMA],
        input_output_aliases={len(parts): 0} if given else {},
        compiler_params=params(),
        cost_estimate=SMALL_COST,
    )(*parts, *given)


def per_device(grad_out, activations, grad_dither, hidden_dither, feature_dither):
    owners = lax.axis_size("dp")
    own_rows = grad_out.shape[1] // owners
    unit_count = activations.shape[1]
    me = lax.axis_index("dp").astype(jnp.int32)
    cores = lax.axis_size("tensor")
    core = lax.axis_index("tensor").astype(jnp.int32)
    pair_bit, half_bit = 1, 2
    lines = [[i for i in range(owners) if i % 4 == r] for r in range(4)]

    def exchange(value, bit):
        return lax.ppermute(value, "dp", [(i, i ^ bit) for i in range(owners)])

    def over_tokens(values):
        if cores == 2:
            return [values, lax.ppermute(values, "tensor", [(0, 1), (1, 0)])]
        return [lax.all_gather(values, "tensor", axis=2, tiled=True)]

    spans, at = [], 0
    chunks, last = chunks_of(unit_count)
    for c in (*chunks, *last):
        spans.append((at, c * LANES))
        at += c * LANES
    spans, last_spans = spans[: len(chunks)], spans[len(chunks) :]
    last_span = (last_spans[0][0], sum(width for _, width in last_spans))

    place = jnp.arange(owners // 4, dtype=jnp.int32)
    mine = 4 * place + me % 4
    owner = jnp.concatenate([mine ^ half_bit, mine])

    last_bit = 4
    last_bits = [b for b in (1 << i for i in range(owners.bit_length() - 1)) if b != last_bit]
    order = relative_order(last_bits)
    order = order[len(order) // 2 :] + order[: len(order) // 2]
    last_owner = jnp.array(order, jnp.int32) ^ me
    last_place = jnp.arange(owners // 4, dtype=jnp.int32)

    dithers = jnp.concatenate([hidden_dither, feature_dither], axis=1)
    dithers_other = exchange(dithers, pair_bit)
    last_dithers = exchange(dithers, last_bit)
    *first, last_cut = cut_columns(activations, [*spans[:2], last_span], [dithers])
    cuts = dict(enumerate(first))
    last_acts = exchange(last_cut, last_bit)
    acts_other = {key: exchange(values, pair_bit) for key, values in cuts.items()}
    y_send = code_rows(
        owner ^ pair_bit, grad_out, grad_dither, own_rows, [cuts[0], dithers_other, last_dithers]
    )
    y_other = exchange(y_send, pair_bit)
    y_mine = code_rows(owner, grad_out, grad_dither, own_rows, [y_send])
    y0 = over_tokens(y_mine)
    last_y_send = code_rows(last_owner ^ last_bit, grad_out, grad_dither, own_rows, [y_mine])
    last_y_other = exchange(last_y_send, last_bit)
    last_y_mine = code_rows(last_owner, grad_out, grad_dither, own_rows, [last_y_send])
    y1 = over_tokens(y_other)

    def halve_all(bit, after):
        for at, (last_keep, last_come) in enumerate(last_parts):
            cost = LARGE_COST if at else SMALL_COST
            last_send, last_keep = halve(last_keep, last_come, after, cost)
            last_parts[at] = [last_keep, exchange(last_send, bit)]
            after = [last_send]
        return after

    result, waiting, last_parts = None, [], []
    out_shape = jax.ShapeDtypeStruct((own_rows, unit_count), jnp.float32)
    after, keep, come = [last_y_mine, last_acts], None, None
    last_at = 3
    for chunk in range(len(spans) + 1):
        keep_now = come_now = None
        if chunk < len(spans):
            start, width = spans[chunk]
            ahead = spans[chunk + 2 : chunk + 3]
            if chunk == 2:
                after = after + [last_y_other]
            send, keep_now, *cut = pair_terms(
                owner, place, core, y0, y1, activations, cuts.pop(chunk), acts_other.pop(chunk),
                [dithers, dithers_other], start, width, 0, ahead, after,
            )
            come_now = exchange(send, half_bit)
            for columns in cut:
                cuts[chunk + 2] = columns
                acts_other[chunk + 2] = exchange(columns, pair_bit)
            after = [send]
            if chunk == 1:
                last_y1 = over_tokens(hold(last_y_other, after))
            if chunk == last_at:
                last_y0 = over_tokens(last_y_mine)
                for block, (last_start, last_width) in enumerate(last_spans):
                    last_send, last_keep = pair_terms(
                        last_owner, last_place, core, last_y0, last_y1, activations, last_cut,
                        last_acts, [dithers, last_dithers], last_start, last_width, block, [], after,
                    )
                    last_parts.append([last_keep, exchange(last_send, last_bits[0])])
                    after = [last_send]
        else:
            after = halve_all(last_bits[1], after)
        if chunk:
            cost = LARGE_COST if chunk == len(spans) else SMALL_COST
            terms = add_up(keep, come, after, cost)
            after = [terms]
            waiting.append((spans[chunk - 1][0], [lax.psum_scatter(
                terms, "dp", scatter_dimension=0, axis_index_groups=lines, tiled=True
            )]))
        keep, come = keep_now, come_now
    for bit in last_bits[2:]:
        after = halve_all(bit, after)
    waiting += [(start, parts) for (start, _), parts in zip(last_spans, last_parts)]
    for start, parts in waiting:
        result = finish(start, parts, result, out_shape)
    return result


def solution(mesh):
    placed = (
        P(("dp", "tensor"), None),
        P("dp", "tensor"),
        P(("dp", "tensor"), None),
        P("dp", "tensor"),
        P("dp", None),
    )
    return jax.shard_map(
        per_device, mesh=mesh, in_specs=placed, out_specs=P("dp", "tensor"), check_vma=False
    )
```

```python
import jax
import jax.numpy as jnp
from jax import lax
from jax.experimental import pallas as pl
from jax.experimental.pallas import tpu as pltpu
from jax.sharding import PartitionSpec as P

BLOCK = 128
Y_LEVELS = 8
W_LEVELS = 7
EPSILON = 1e-06
LANES = 128
LARGE_COST = pl.CostEstimate(flops=2 * 10**11, bytes_accessed=1, transcendentals=0)
SMALL_COST = pl.CostEstimate(flops=1, bytes_accessed=1, transcendentals=0)
ANYWHERE = pl.BlockSpec(memory_space=pl.ANY)

CHUNKS = (4, 6, 10, 10, 10)
LAST = (8, 8)


def chunks_of(unit_count):
    units = unit_count // LANES
    if units == sum(CHUNKS) + sum(LAST):
        return CHUNKS, LAST
    last = max(units // 8, 1)
    rest = units - 2 * last
    return (rest - 4 * (rest // 5),) + (rest // 5,) * 4, (last, last)


def params():
    return pltpu.CompilerParams(vmem_limit_bytes=64 * 1024 * 1024)


def code_rows(order, grad_out, grad_dither, own_rows, after=()):
    row_count = grad_out.shape[0]
    steps = order.shape[0]
    spec = pl.BlockSpec((row_count, own_rows), lambda i, order: (0, order[i]))

    def body(order_ref, grad_ref, dither_ref, *rest):
        for start in range(0, own_rows, BLOCK):
            grad = grad_ref[:, start : start + BLOCK].astype(jnp.float32)
            top = jnp.max(jnp.abs(grad), axis=1, keepdims=True)
            scale = ((top + EPSILON) / Y_LEVELS).astype(jnp.bfloat16).astype(jnp.float32)
            value = grad + dither_ref[:, start : start + BLOCK] * scale
            rest[-1][0, start : start + BLOCK, :] = value.astype(jnp.bfloat16).T

    return pl.pallas_call(
        body,
        grid_spec=pltpu.PrefetchScalarGridSpec(
            num_scalar_prefetch=1,
            grid=(steps,),
            in_specs=[spec, spec] + [ANYWHERE] * len(after),
            out_specs=pl.BlockSpec((1, own_rows, row_count), lambda i, order: (i, 0, 0)),
        ),
        out_shape=jax.ShapeDtypeStruct((steps, own_rows, row_count), jnp.bfloat16),
        compiler_params=params(),
        cost_estimate=SMALL_COST,
    )(order, grad_out, grad_dither, *after)


def column_block(rows, start, width):
    return pl.BlockSpec((pl.Element(rows), pl.Element(width)), lambda i, *_: (i * rows, start))


def cut_columns(values, spans, after=()):
    rows = values.shape[0]
    steps = 4

    def body(*refs):
        for in_ref, out_ref in zip(refs, refs[-len(spans) :]):
            out_ref[...] = in_ref[...]

    return pl.pallas_call(
        body,
        grid=(steps,),
        in_specs=[column_block(rows // steps, *span) for span in spans] + [ANYWHERE] * len(after),
        out_specs=[pl.BlockSpec((rows // steps, width), lambda i: (i, 0)) for _, width in spans],
        out_shape=[jax.ShapeDtypeStruct((rows, width), values.dtype) for _, width in spans],
        compiler_params=params(),
        cost_estimate=SMALL_COST,
    )(*[values] * len(spans), *after)


def joined(core, pieces):
    if len(pieces) == 1:
        return pieces[0][0]
    mine, other = (p[0] for p in pieces)
    return jnp.where(
        core == 0, jnp.concatenate([mine, other], axis=1), jnp.concatenate([other, mine], axis=1)
    )


def group_terms(y_block, acts, hidden, feature):
    rows, width = y_block.shape[0], acts.shape[1]
    partial = jnp.dot(y_block, acts, preferred_element_type=jnp.float32)
    column = jnp.broadcast_to(feature, (LANES, rows)).T
    wide = jnp.concatenate([column] * (width // LANES), axis=1)
    out = []
    for start in range(0, rows, BLOCK):
        piece = partial[start : start + BLOCK]
        top = jnp.max(jnp.abs(piece), axis=0, keepdims=True)
        scale = ((top + EPSILON) / W_LEVELS).astype(jnp.bfloat16).astype(jnp.float32)
        out.append(piece + (wide[start : start + BLOCK] + hidden) * scale)
    return jnp.concatenate(out, axis=0)


def pair_terms(
    owner, place, core, y0, y1, acts, acts0, acts1, dithers, start, width, block, ahead, after, cost
):
    steps, own_rows = y0[0].shape[:2]
    tokens, units = acts.shape
    half = steps // 2
    count, both = len(y0), len(y0) + len(y1)

    def body(table_ref, *refs):
        refs = list(refs)
        y0_refs, y1_refs = refs[:count], refs[count : both]
        a0_ref, a1_ref, h0_ref, h1_ref, f0_ref, f1_ref = refs[both : both + 6]
        cut_refs = refs[both + 6 : both + 6 + len(ahead)]
        outs = refs[both + 6 + len(ahead) + len(after) :]
        core = table_ref[steps + half]
        for cut_ref, out_ref in zip(cut_refs, outs[2:]):
            out_ref[...] = cut_ref[...]
        columns = slice(start, start + width)
        mine = group_terms(joined(core, y0_refs), a0_ref[...], h0_ref[:, columns], f0_ref[...])
        other = group_terms(joined(core, y1_refs), a1_ref[...], h1_ref[:, columns], f1_ref[...])
        total = (mine + other).astype(jnp.bfloat16)
        step = pl.program_id(0)

        @pl.when(step < half)
        def _():
            outs[0][...] = total

        @pl.when(step >= half)
        def _():
            outs[1][...] = total


    y0_specs, y1_specs = (
        [pl.BlockSpec((1, own_rows, y.shape[2]), lambda i, t: (i, 0, 0)) for y in ys] for ys in (y0, y1)
    )
    f_spec = pl.BlockSpec((1, own_rows), lambda i, t: (0, units // own_rows + t[i]))
    h_spec = pl.BlockSpec((1, dithers[0].shape[1]), lambda i, t: (0, 0))
    a_spec = pl.BlockSpec((tokens, width), lambda i, t: (0, block))
    out_specs = [
        pl.BlockSpec((own_rows, width), lambda i, t: (t[steps + jnp.minimum(i, half - 1)], 0)),
        pl.BlockSpec((own_rows, width), lambda i, t: (t[steps + jnp.maximum(i - half, 0)], 0)),
    ]
    out_shape = [jax.ShapeDtypeStruct((half * own_rows, width), jnp.bfloat16)] * 2
    for _, cut_width in ahead:
        out_specs.append(pl.BlockSpec((tokens // steps, cut_width), lambda i, t: (i, 0)))
        out_shape.append(jax.ShapeDtypeStruct((tokens, cut_width), acts.dtype))
    return pl.pallas_call(
        body,
        grid_spec=pltpu.PrefetchScalarGridSpec(
            num_scalar_prefetch=1,
            grid=(steps,),
            in_specs=[*y0_specs, *y1_specs, a_spec, a_spec, h_spec, h_spec, f_spec, f_spec]
            + [column_block(tokens // steps, *span) for span in ahead]
            + [ANYWHERE] * len(after),
            out_specs=out_specs,
        ),
        out_shape=out_shape,
        compiler_params=params(),
        cost_estimate=cost,
    )(
        jnp.concatenate([owner, place, core[None]]),
        *y0, *y1, acts0, acts1, *dithers, *dithers, *[acts] * len(ahead), *after,
    )


def add_up(keep, come, after, cost):
    rows, width = keep.shape

    def body(keep_ref, come_ref, *rest):
        total = keep_ref[...].astype(jnp.float32) + come_ref[...].astype(jnp.float32)
        rest[-1][...] = total.astype(jnp.bfloat16)

    spec = pl.BlockSpec((2 * LANES, width), lambda i: (i, 0))
    return pl.pallas_call(
        body,
        grid=(rows // (2 * LANES),),
        in_specs=[spec, spec] + [ANYWHERE] * len(after),
        out_specs=spec,
        out_shape=jax.ShapeDtypeStruct((rows, width), jnp.bfloat16),
        compiler_params=params(),
        cost_estimate=cost,
    )(keep, come, *after)


def halve(keep, come, after, cost):
    rows, width = keep.shape
    half = rows // (2 * LANES)

    def body(keep_ref, come_ref, *rest):
        total = keep_ref[...].astype(jnp.float32) + come_ref[...].astype(jnp.float32)
        step = pl.program_id(0)

        @pl.when(step < half)
        def _():
            rest[-2][...] = total.astype(jnp.bfloat16)

        @pl.when(step >= half)
        def _():
            rest[-1][...] = total.astype(jnp.bfloat16)

    spec = pl.BlockSpec((LANES, width), lambda i: (jnp.where(i < half, i + half, i - half), 0))
    return pl.pallas_call(
        body,
        grid=(2 * half,),
        in_specs=[spec, spec] + [ANYWHERE] * len(after),
        out_specs=[
            pl.BlockSpec((LANES, width), lambda i: (jnp.minimum(i, half - 1), 0)),
            pl.BlockSpec((LANES, width), lambda i: (jnp.maximum(i - half, 0), 0)),
        ],
        out_shape=[jax.ShapeDtypeStruct((rows // 2, width), jnp.bfloat16)] * 2,
        compiler_params=params(),
        cost_estimate=cost,
    )(keep, come, *after)


def hold(value, after):
    def body(*refs):
        del refs

    return pl.pallas_call(
        body,
        in_specs=[ANYWHERE] * (1 + len(after)),
        out_specs=ANYWHERE,
        out_shape=jax.ShapeDtypeStruct(value.shape, value.dtype),
        input_output_aliases={0: 0},
        compiler_params=params(),
        cost_estimate=SMALL_COST,
    )(value, *after)


def relative_order(bits):
    order = [0]
    for bit in reversed(bits):
        order = order + [bit | r for r in order]
    return order


def finish(start, parts, result, out_shape):
    own_rows, width = parts[0].shape
    given = [] if result is None else [result]

    def body(*refs):
        out_ref, held, sem = refs[-3:]
        total = refs[0][...].astype(jnp.float32)
        for ref in refs[1 : len(parts)]:
            total = total + ref[...].astype(jnp.float32)
        held[...] = total
        copy = pltpu.make_async_copy(held, out_ref.at[:, pl.ds(start, width)], sem)
        copy.start()
        copy.wait()

    return pl.pallas_call(
        body,
        in_specs=[pl.BlockSpec(memory_space=pltpu.VMEM)] * len(parts) + [ANYWHERE] * len(given),
        out_specs=ANYWHERE,
        out_shape=out_shape,
        scratch_shapes=[pltpu.VMEM((own_rows, width), jnp.float32), pltpu.SemaphoreType.DMA],
        input_output_aliases={len(parts): 0} if given else {},
        compiler_params=params(),
        cost_estimate=SMALL_COST,
    )(*parts, *given)


def per_device(grad_out, activations, grad_dither, hidden_dither, feature_dither):
    owners = lax.axis_size("dp")
    own_rows = grad_out.shape[1] // owners
    unit_count = activations.shape[1]
    me = lax.axis_index("dp").astype(jnp.int32)
    cores = lax.axis_size("tensor")
    core = lax.axis_index("tensor").astype(jnp.int32)
    pair_bit, half_bit = 1, 2
    lines = [[i for i in range(owners) if i % 4 == r] for r in range(4)]

    def exchange(value, bit):
        return lax.ppermute(value, "dp", [(i, i ^ bit) for i in range(owners)])

    def over_tokens(values):
        if cores == 2:
            return [values, lax.ppermute(values, "tensor", [(0, 1), (1, 0)])]
        return [lax.all_gather(values, "tensor", axis=2, tiled=True)]

    spans, at = [], 0
    chunks, last = chunks_of(unit_count)
    for c in (*chunks, *last):
        spans.append((at, c * LANES))
        at += c * LANES
    spans, last_spans = spans[: len(chunks)], spans[len(chunks) :]
    last_span = (last_spans[0][0], sum(width for _, width in last_spans))

    place = jnp.arange(owners // 4, dtype=jnp.int32)
    mine = 4 * place + me % 4
    owner = jnp.concatenate([mine ^ half_bit, mine])

    last_bit = 4
    last_bits = [b for b in (1 << i for i in range(owners.bit_length() - 1)) if b != last_bit]
    order = relative_order(last_bits)
    order = order[len(order) // 2 :] + order[: len(order) // 2]
    last_owner = jnp.array(order, jnp.int32) ^ me
    last_place = jnp.arange(owners // 4, dtype=jnp.int32)

    dithers = jnp.concatenate([hidden_dither, feature_dither], axis=1)
    dithers_other = exchange(dithers, pair_bit)
    last_dithers = exchange(dithers, last_bit)
    *first, last_cut = cut_columns(activations, [*spans[:2], last_span], [dithers])
    cuts = dict(enumerate(first))
    last_acts = exchange(last_cut, last_bit)
    acts_other = {key: exchange(values, pair_bit) for key, values in cuts.items()}
    y_send = code_rows(
        owner ^ pair_bit, grad_out, grad_dither, own_rows, [cuts[0], dithers_other, last_dithers]
    )
    y_other = exchange(y_send, pair_bit)
    y_mine = code_rows(owner, grad_out, grad_dither, own_rows, [y_send])
    y0 = over_tokens(y_mine)
    last_y_send = code_rows(last_owner ^ last_bit, grad_out, grad_dither, own_rows, [y_mine])
    last_y_other = exchange(last_y_send, last_bit)
    last_y_mine = code_rows(last_owner, grad_out, grad_dither, own_rows, [last_y_send])
    y1 = over_tokens(y_other)

    def halve_all(bit, after):
        for at, (last_keep, last_come) in enumerate(last_parts):
            cost = LARGE_COST if at else SMALL_COST
            last_send, last_keep = halve(last_keep, last_come, after, cost)
            last_parts[at] = [last_keep, exchange(last_send, bit)]
            after = [last_send]
        return after

    def last_terms(block, after):
        last_start, last_width = last_spans[block]
        last_send, last_keep = pair_terms(
            last_owner, last_place, core, last_y0, last_y1, activations, last_cut, last_acts,
            [dithers, last_dithers], last_start, last_width, block, [], after, SMALL_COST,
        )
        last_parts.append([last_keep, exchange(last_send, last_bits[0])])
        return [last_send]

    result, waiting, last_parts = None, [], []
    out_shape = jax.ShapeDtypeStruct((own_rows, unit_count), jnp.float32)
    after, keep, come = [last_y_mine, last_acts], None, None
    last_at = 3
    for chunk in range(len(spans) + 1):
        keep_now = come_now = None
        if chunk < len(spans):
            start, width = spans[chunk]
            ahead = spans[chunk + 2 : chunk + 3]
            if chunk == 2:
                after = after + [last_y_other]
            send, keep_now, *cut = pair_terms(
                owner, place, core, y0, y1, activations, cuts.pop(chunk), acts_other.pop(chunk),
                [dithers, dithers_other], start, width, 0, ahead, after, LARGE_COST,
            )
            come_now = exchange(send, half_bit)
            for columns in cut:
                cuts[chunk + 2] = columns
                acts_other[chunk + 2] = exchange(columns, pair_bit)
            after = [send]
            if chunk == 1:
                last_y1 = over_tokens(hold(last_y_other, after))
            if chunk == last_at:
                last_y0 = over_tokens(last_y_mine)
                after = last_terms(0, after)
        else:
            after = halve_all(last_bits[1], after)
        if chunk:
            cost = LARGE_COST if chunk == len(spans) else SMALL_COST
            terms = add_up(keep, come, after, cost)
            after = [terms]
            waiting.append((spans[chunk - 1][0], [lax.psum_scatter(
                terms, "dp", scatter_dimension=0, axis_index_groups=lines, tiled=True
            )]))
        if chunk == last_at:
            after = last_terms(1, after)
        keep, come = keep_now, come_now
    for bit in last_bits[2:]:
        after = halve_all(bit, after)
    waiting += [(start, parts) for (start, _), parts in zip(last_spans, last_parts)]
    for start, parts in waiting:
        result = finish(start, parts, result, out_shape)
    return result


def solution(mesh):
    placed = (
        P(("dp", "tensor"), None),
        P("dp", "tensor"),
        P(("dp", "tensor"), None),
        P("dp", "tensor"),
        P("dp", None),
    )
    return jax.shard_map(
        per_device, mesh=mesh, in_specs=placed, out_specs=P("dp", "tensor"), check_vma=False
    )
```
